32 devices in a mesh: energy: 8 (over z, y), slab: 4 (over x, core).
Axes of the slice: x: 2, y: 2, z: 4, core: 2. Of those that a mesh axis runs over, the one named last changes fastest.
Arguments:
- energy_real: float32 [32], P('energy'), may hold values from -2 to 2
- energy_imag: float32 [32], P('energy'), may hold values from 1 to 2
- potential: float32 [4, 256], P('slab'), may hold values from -1.5 to 1.5
- onsite: float32 [4, 2, 256, 256], P('slab'), may hold values from -0.078125 to 0.078125
- coupling: float32 [4, 2, 256, 256], P('slab'), may hold values from -1.1 to 1.1
- deform: float32 [4, 256, 256], P('slab'), may hold values from 0.2 to 1
- offsets: int32 [8], replicated, may hold values from -8 to 8, as said below
- weights: int32 [8], replicated, may hold values from 8 to 40
Outputs:
- green: float32 [32, 4, 2, 256, 256], P('energy', 'slab')
- self_energy: float32 [32, 4, 2, 256, 256], P('energy', 'slab')
The draws below stay inside these ranges and needn't reach their ends.
Inputs may be any that keep to these rules, and one draw needn't show every extreme that they name: Eight offsets; -8 and 8 are always among them.
All inputs are finite; a program needn't handle non-finite values.
Results may differ from the reference program's by a relative error of at most 0.0001.
Values sent between devices are 32-bit elements; how exact they have to be, the bound alone decides.
A program may use at most 128 MiB of HBM per device.

```python
import math
import jax
import jax.numpy as jnp
from jax import lax

M = 256
E_DEV = 4
OFFSETS = 8
SWEEPS = 3
OUTER = 2
NEWTON = 2
ENERGIES = 32
SLABS = 4


def draw_offsets(key, part):
    values = jax.random.randint(key, (OFFSETS,), -2 * E_DEV, 2 * E_DEV + 1)
    position = jnp.arange(OFFSETS)
    values = jnp.where(position == 0, -2 * E_DEV, jnp.where(position == 1, 2 * E_DEV, values))
    order = jax.random.permutation(jax.random.fold_in(key, 7), OFFSETS)
    return values[order].astype(jnp.int32)


def draw_coupling(key, part):
    key_size = jax.random.fold_in(key, 11)
    key_angle = jax.random.fold_in(key, 12)
    key_jitter = jax.random.fold_in(key, 13)
    shape = (SLABS, 2, M, M)
    magnitude = jnp.exp(jax.random.uniform(key_size, (SLABS, M), jnp.float32, math.log(0.5), math.log(0.95)))
    jitter = jnp.clip(jax.random.normal(key_jitter, shape, jnp.float32), -4.0, 4.0)
    angles = jax.random.uniform(key_angle, (SLABS, M), jnp.float32, -math.pi, math.pi)
    spread = 0.25 / math.sqrt(2.0 * M)
    identity = jnp.eye(M, dtype=jnp.float32)
    diagonal_real = (magnitude * jnp.cos(angles))[:, :, None] * identity
    diagonal_imag = (magnitude * jnp.sin(angles))[:, :, None] * identity
    return (jnp.stack([diagonal_real, diagonal_imag], axis=1) + spread * jitter).astype(jnp.float32)


def set_ends(values, rng, low, largest):
    extent = values.shape
    index_at = [jax.random.randint(jax.random.fold_in(rng, axis), (), 0, extent[axis]) for axis in range(len(extent))]
    values = values.at[tuple(index_at)].set(low)
    longest = extent.index(max(extent))
    index_at[longest] = (index_at[longest] + 1) % extent[longest]
    return values.at[tuple(index_at)].set(largest)


def steps_of(own_key, shape, shards, smallest, largest):
    level, own = 1.0, jax.random.fold_in(own_key, 6)
    for dim, shards_of in shards:
        heights = jnp.exp(jax.random.uniform(jax.random.fold_in(own, dim), (shards_of,), jnp.float32, smallest / len(shards), largest / len(shards)))
        level = level * jnp.repeat(heights, shape[dim] // shards_of).reshape([-1 if axis == dim else 1 for axis in range(len(shape))])
    return level


def gaussian(stream_key, shape, deviation, reach, split=(), kind=jnp.bfloat16):
    gain = steps_of(stream_key, shape, split, -0.22, 0.18) if split else 1.0
    entries = jax.random.normal(stream_key, shape, jnp.float32) * deviation * gain
    return jnp.minimum(jnp.maximum(entries, -reach), reach).astype(kind)


def setup_inputs(seed: int = 0) -> dict:
    arg_keys = jax.random.split(jax.random.key(seed), 9)
    energy_real = jnp.clip(jax.random.uniform(arg_keys[0], (ENERGIES,), jnp.float32, -2.0, 2.0) * steps_of(arg_keys[0], (ENERGIES,), ((0, 8),), -0.4, 0.0), -2.0, 2.0)
    energy_imag = jnp.clip(jnp.exp(math.log(2.0) - 0.6931472 * jax.random.uniform(arg_keys[1], (ENERGIES,), jnp.float32) ** steps_of(arg_keys[1], (ENERGIES,), ((0, 8),), -0.2, 0.2)), 1.0, 2.0)
    potential = jnp.clip(jax.random.uniform(arg_keys[2], (SLABS, M), jnp.float32, -1.5, 1.5) * steps_of(arg_keys[2], (SLABS, M), ((0, 4),), -0.4, 0.0), -1.5, 1.5)
    onsite = gaussian(arg_keys[3], (SLABS, 2, M, M), (25 * M) ** -0.5, 0.078125, ((0, 4),), jnp.float32)
    coupling = draw_coupling(jax.random.fold_in(arg_keys[8], 71), 0)
    deform = jnp.clip(0.2 + 0.8 * jax.random.uniform(arg_keys[5], (SLABS, M, M), jnp.float32) ** steps_of(arg_keys[5], (SLABS, M, M), ((0, 4),), -0.2, 0.2), 0.2, 1.0)
    offsets = draw_offsets(jax.random.fold_in(arg_keys[8], 71), 0)
    weights = set_ends(jax.random.randint(arg_keys[7], (OFFSETS,), 8, 41), jax.random.fold_in(arg_keys[7], 1), 8, 40).astype(jnp.int32)
    return dict(energy_real=energy_real, energy_imag=energy_imag, potential=potential, onsite=onsite, coupling=coupling, deform=deform, offsets=offsets, weights=weights)


def matmul_high(left, right):
    return jnp.matmul(left, right, precision=lax.Precision.HIGHEST)


def complex_mul(left, right):
    left_real, left_imag = left[..., 0, :, :], left[..., 1, :, :]
    right_real, right_imag = right[..., 0, :, :], right[..., 1, :, :]
    real_part = matmul_high(left_real, right_real) - matmul_high(left_imag, right_imag)
    imag_part = matmul_high(left_real, right_imag) + matmul_high(left_imag, right_real)
    return jnp.stack([real_part, imag_part], axis=-3)


def adjoint(matrix):
    return jnp.stack([jnp.swapaxes(matrix[..., 0, :, :], -1, -2), -jnp.swapaxes(matrix[..., 1, :, :], -1, -2)], axis=-3)


def invert(matrix_real, matrix_imag):
    block_order = matrix_real.shape[-1]
    identity = jnp.eye(block_order, dtype=jnp.float32)
    diagonal_real = jnp.diagonal(matrix_real, axis1=-2, axis2=-1)
    diagonal_imag = jnp.diagonal(matrix_imag, axis1=-2, axis2=-1)
    modulus = diagonal_real * diagonal_real + diagonal_imag * diagonal_imag
    inverse_real = diagonal_real / modulus
    inverse_imag = -diagonal_imag / modulus
    column_real = inverse_real[..., None, :]
    column_imag = inverse_imag[..., None, :]
    product_real = matrix_real * column_real - matrix_imag * column_imag
    product_imag = matrix_real * column_imag + matrix_imag * column_real
    remainder_real = 2.0 * identity - product_real
    remainder_imag = -product_imag
    row_real = inverse_real[..., :, None]
    row_imag = inverse_imag[..., :, None]
    estimate = jnp.stack([row_real * remainder_real - row_imag * remainder_imag, row_real * remainder_imag + row_imag * remainder_real], axis=-3)
    matrix = jnp.stack([matrix_real, matrix_imag], axis=-3)
    for newton_step in range(NEWTON - 1):
        product = complex_mul(matrix, estimate)
        remainder = jnp.stack([2.0 * identity - product[..., 0, :, :], -product[..., 1, :, :]], axis=-3)
        estimate = complex_mul(estimate, remainder)
    return estimate


def reference(energy_real, energy_imag, potential, onsite, coupling, deform, offsets, weights):
    block_order = onsite.shape[-1]
    energy_count = energy_real.shape[0]
    identity = jnp.eye(block_order, dtype=jnp.float32)
    base_real = energy_real[:, None, None, None] * identity - (potential[:, :, None] * identity)[None] - onsite[None, :, 0]
    base_imag = energy_imag[:, None, None, None] * identity - onsite[None, :, 1]
    coupling_adj = adjoint(coupling)
    green = jnp.zeros((energy_count,) + onsite.shape, jnp.float32)
    sigma = jnp.zeros((energy_count,) + onsite.shape, jnp.float32)
    row_index = jnp.arange(energy_count, dtype=jnp.int32)[:, None, None]
    col_index = jnp.arange(energy_count, dtype=jnp.int32)[None, :, None]
    target = row_index + offsets[None, None, :]
    table = jnp.sum(jnp.where(col_index == target, weights.astype(jnp.float32)[None, None, :] / 128.0, jnp.float32(0.0)), axis=-1)
    for outer_step in range(OUTER):
        for sweep_step in range(SWEEPS):
            incoming = jnp.concatenate([jnp.zeros_like(green[:, :1]), green[:, :-1]], axis=1)
            couple = complex_mul(complex_mul(coupling[None], incoming), coupling_adj[None])
            green = invert(base_real - sigma[:, :, 0] - couple[:, :, 0], base_imag - sigma[:, :, 1] - couple[:, :, 1])
        summed = jnp.tensordot(table, green, axes=1, precision=lax.Precision.HIGHEST)
        sigma = deform[None, :, None] * summed
    return green, sigma
```

```python
import functools

import jax
import jax.numpy as jnp
from jax import lax
from jax.experimental import pallas as pl
from jax.experimental.pallas import tpu as pltpu
from jax.sharding import PartitionSpec as P

MESH = pl.DeviceIdType.MESH
CHUNKS = 4
F32 = jnp.float32
BF16 = jnp.bfloat16


def split(value):
    high = value.astype(BF16)
    return high, (value - high.astype(F32)).astype(BF16)


def dot(left, right):
    return jnp.dot(left, right, preferred_element_type=F32)


def dot3(left, right):
    return dot(left[0], right[0]) + (dot(left[0], right[1]) + dot(left[1], right[0]))


def put_split(ref, place, value):
    ref[place], ref[place + 1] = split(value)


def get_split(ref, place):
    return ref[place], ref[place + 1]


def kernel(
    n, slabs, er_ref, ei_ref, table_ref, base_ref, coupling_ref, deform_ref,
    green_ref, sigma_ref,
    big, couple, c_left, c_right, work, work2, pair, from_low, from_high, to_low, to_high,
    slot_send, slot_recv, pair_send, pair_recv, low_send, low_recv, high_send, high_recv,
):
    energies = er_ref.shape[0]
    order = base_ref.shape[-1]
    rows = order // CHUNKS
    me = lax.axis_index("energy")
    q = lax.axis_index("slab")
    side = lax.rem(me, 2)
    partner = me + 1 - 2 * side
    has_low, has_high = me >= 2, me + 2 < n

    def at(energy, slab):
        return {"energy": energy, "slab": slab}

    barrier = pltpu.get_barrier_semaphore()

    def greet(present, energy, slab):
        @pl.when(present)
        def _():
            pl.semaphore_signal(barrier, inc=1, device_id=at(energy, slab), device_id_type=MESH)

    pl.semaphore_signal(barrier, inc=1, device_id=at(partner, q), device_id_type=MESH)
    greet(has_low, me - 2, q)
    greet(has_high, me + 2, q)
    greet(q >= 1, me, q - 1)
    greet(q + 1 < slabs, me, q + 1)

    sigma_ref[...] = jnp.zeros_like(sigma_ref)
    for part in range(2):
        put_split(c_left, 2 * part, coupling_ref[part])
        put_split(c_right, 2 * part, coupling_ref[part].T)

    peers = 1
    for present in (has_low, has_high, q >= 1, q + 1 < slabs):
        peers = peers + jnp.where(present, 1, 0)
    pl.semaphore_wait(barrier, peers)

    identity_mask = lax.broadcasted_iota(jnp.int32, (order, order), 0) == lax.broadcasted_iota(
        jnp.int32, (order, order), 1
    )

    def slot_copy(source, slot, energy):
        return pltpu.make_async_remote_copy(
            src_ref=big.at[source, energy],
            dst_ref=big.at[6 + slot, energy],
            send_sem=slot_send.at[slot, energy],
            recv_sem=slot_recv.at[slot, energy],
            device_id=at(me, lax.rem(q + 1, slabs)),
            device_id_type=MESH,
        )

    middle = max(slabs - 2, 1)

    def compute(outer, sweep, energy):
        local = (outer == 0) & (sweep == 1)
        source = jnp.where(local, 0, 6 + outer * sweep)
        coupled = (q >= 1) & jnp.logical_not((outer == 0) & (sweep == 0))

        @pl.when(coupled & jnp.logical_not(local))
        def _():
            slot_copy(0, outer * sweep, energy).wait_recv()

        @pl.when(coupled)
        def _():
            put_split(work, 0, big[source, energy, 0])
            put_split(work, 2, big[source, energy, 1])
            cr, ci = get_split(c_left, 0), get_split(c_left, 2)
            gr, gi = get_split(work, 0), get_split(work, 2)
            tr = split(dot3(cr, gr) - dot3(ci, gi))
            ti = split(dot3(cr, gi) + dot3(ci, gr))
            dr, di = get_split(c_right, 0), get_split(c_right, 2)
            couple[0] = dot3(tr, dr) + dot3(ti, di)
            couple[1] = dot3(ti, dr) - dot3(tr, di)

        @pl.when(jnp.logical_not(coupled))
        def _():
            couple[...] = jnp.zeros_like(couple)

        which = jnp.where((outer == 0) & (sweep == 0), 1, 0)
        ar = base_ref[which, 0] - sigma_ref[energy, 0, 0] - couple[0]
        ai = base_ref[which, 1] - sigma_ref[energy, 0, 1] - couple[1]
        dr = jnp.where(identity_mask, ar + er_ref[energy], 0.0)
        di = jnp.where(identity_mask, ai + ei_ref[energy], 0.0)

        def reciprocal(axis):
            r, i = jnp.sum(dr, axis=axis, keepdims=True), jnp.sum(di, axis=axis, keepdims=True)
            modulus = r * r + i * i
            return r / modulus, -i / modulus

        col_r, col_i = reciprocal(0)
        row_r, row_i = reciprocal(1)
        off_r = jnp.where(identity_mask, 0.0, ar)
        off_i = jnp.where(identity_mask, 0.0, ai)
        w_r = off_r * col_r - off_i * col_i
        w_i = off_r * col_i + off_i * col_r
        couple[0], couple[1] = w_r, w_i
        put_split(work, 0, w_r)
        put_split(work, 2, w_i)
        wr, wi = get_split(work, 0), get_split(work, 2)
        s_r = dot3(wr, wr) - dot3(wi, wi)
        s_i = dot3(wr, wi) + dot3(wi, wr)
        put_split(work2, 0, s_r)
        put_split(work2, 2, s_i)
        sr, si = get_split(work2, 0), get_split(work2, 2)
        y_r = s_r - couple[0] - (dot3(wr, sr) - dot3(wi, si)) + jnp.where(identity_mask, 1.0, 0.0)
        y_i = s_i - couple[1] - (dot3(wr, si) + dot3(wi, sr))
        target = 3 * outer + sweep
        big[target, energy, 0] = row_r * y_r - row_i * y_i
        big[target, energy, 1] = row_r * y_i + row_i * y_r

        slot = jnp.where(outer == 0, 0, sweep + 1)
        first = (outer == 0) & (sweep == 1)
        second = (outer == 1) & (sweep == 0) & (q + 1 <= middle)
        third = (outer == 1) & (sweep == 1)

        @pl.when((q + 1 < slabs) & (first | second | third))
        def _():
            slot_copy(target, slot, energy).start()

    def pair_copy(outer, final, c):
        cut = pl.ds(c * rows, rows)
        return pltpu.make_async_remote_copy(
            src_ref=big.at[final, :, :, cut],
            dst_ref=pair.at[outer, :, :, cut],
            send_sem=pair_send.at[outer, c],
            recv_sem=pair_recv.at[outer, c],
            device_id=at(partner, q),
            device_id_type=MESH,
        )

    def low_copy(outer, c):
        cut = pl.ds(c * rows, rows)
        return pltpu.make_async_remote_copy(
            src_ref=to_low.at[:, :, cut],
            dst_ref=from_high.at[outer, :, :, cut],
            send_sem=low_send.at[outer, c],
            recv_sem=low_recv.at[outer, c],
            device_id=at(lax.rem(me + n - 2, n), q),
            device_id_type=MESH,
        )

    def high_copy(outer, c):
        cut = pl.ds(c * rows, rows)
        return pltpu.make_async_remote_copy(
            src_ref=to_high.at[:, :, cut],
            dst_ref=from_low.at[outer, :, :, cut],
            send_sem=high_send.at[outer, c],
            recv_sem=high_recv.at[outer, c],
            device_id=at(lax.rem(me + 2, n), q),
            device_id_type=MESH,
        )

    zero_at = 4 * energies - 1
    step_to_partner = energies * (1 - 2 * side)
    strip = 8

    def each_strip(c, body):
        def one(index, carry):
            body(pl.ds(pl.multiple_of(c * rows + index * strip, strip), strip))
            return carry

        lax.fori_loop(0, rows // strip, one, 0)

    def exchange(outer):
        final = jnp.where(outer == 0, jnp.where(q >= 2, 2, 1), 3 + jnp.minimum(q, 2))
        for c in range(CHUNKS):
            pair_copy(outer, final, c).start()
        for c in range(CHUNKS):
            pair_copy(outer, final, c).wait_recv()

            def sums(shift, goal, final=final):
                weight = [
                    [
                        [
                            table_ref[zero_at + shift + b - a + extra]
                            for extra in (0, step_to_partner)
                        ]
                        for b in range(energies)
                    ]
                    for a in range(energies)
                ]

                def body(cut):
                    for part in range(2):
                        own = [big[final, b, part, cut] for b in range(energies)]
                        other = [pair[outer, b, part, cut] for b in range(energies)]
                        for a in range(energies):
                            total = weight[a][0][0] * own[0]
                            for b in range(energies):
                                if b:
                                    total = total + weight[a][b][0] * own[b]
                                total = total + weight[a][b][1] * other[b]
                            goal(a, part, cut, total)

                each_strip(c, body)

            def put_high(a, part, cut, value):
                to_high[a, part, cut] = value

            def put_low(a, part, cut, value):
                to_low[a, part, cut] = value

            def put_own(a, part, cut, value):
                sigma_ref[a, 0, part, cut] = value

            @pl.when(has_high)
            def _():
                sums(-2 * energies, put_high)
                high_copy(outer, c).start()

            @pl.when(has_low)
            def _():
                sums(2 * energies, put_low)
                low_copy(outer, c).start()

            sums(0, put_own)

        for c in range(CHUNKS):

            def add(source):
                def body(cut):
                    for a in range(energies):
                        for part in range(2):
                            sigma_ref[a, 0, part, cut] += source[outer, a, part, cut]

                each_strip(c, body)

            @pl.when(has_low)
            def _():
                high_copy(outer, c).wait_recv()
                add(from_low)

            @pl.when(has_high)
            def _():
                low_copy(outer, c).wait_recv()
                add(from_high)

            def scale(cut):
                level = deform_ref[cut]
                for a in range(energies):
                    for part in range(2):
                        sigma_ref[a, 0, part, cut] = level * sigma_ref[a, 0, part, cut]

            each_strip(c, scale)

        for c in range(CHUNKS):
            pair_copy(outer, final, c).wait_send()

            @pl.when(has_high)
            def _():
                high_copy(outer, c).wait_send()

            @pl.when(has_low)
            def _():
                low_copy(outer, c).wait_send()

    def outer_step(outer, carry):
        def step(j, inner):
            paired = (outer == 0) & (j < 2 * energies)
            sweep = jnp.where(paired, lax.rem(j, 2), lax.div(j, energies))
            energy = jnp.where(paired, lax.div(j, 2), lax.rem(j, energies))
            start = jnp.where(outer == 0, q >= 1, q <= 1)
            mid = (q <= middle) & ((outer == 0) | (q >= 1))
            active = (
                ((sweep == 0) & start) | ((sweep == 1) & mid) | ((sweep == 2) & (q >= 2))
            )

            @pl.when(active)
            def _():
                compute(outer, sweep, energy)

            return inner

        lax.fori_loop(0, 3 * energies, step, 0)
        exchange(outer)
        return carry

    lax.fori_loop(0, 2, outer_step, 0)

    final = 3 + jnp.minimum(q, 2)

    def out(index, carry):
        cut = pl.ds(pl.multiple_of(index * 64, 64), 64)
        for a in range(energies):
            for part in range(2):
                green_ref[a, 0, part, cut] = big[final, a, part, cut]
        return carry

    lax.fori_loop(0, order // 64, out, 0)

    def drain(slot, present):
        @pl.when(present & (q + 1 < slabs))
        def _():
            for energy in range(energies):
                slot_copy(0, slot, energy).wait_send()

    drain(0, q <= middle)
    drain(1, q + 1 <= middle)
    drain(2, (q >= 1) & (q <= middle))


def on_device(n, slabs, energy_real, energy_imag, potential, onsite, coupling, deform, offsets, weights):
    order = onsite.shape[-1]
    energies = energy_real.shape[0]
    base = jnp.stack(
        [-onsite[0, 0] - potential[0][:, None] * jnp.eye(order, dtype=F32), -onsite[0, 1]]
    )
    before = lax.ppermute(base, "slab", [(i, i + 1) for i in range(slabs - 1)])
    gap = jnp.arange(8 * energies - 1, dtype=jnp.int32) - (4 * energies - 1)
    table = jnp.sum(
        jnp.where(gap[:, None] == offsets[None, :], weights.astype(F32)[None, :] / 128.0, 0.0), axis=-1
    )
    shape = (energies, 1, 2, order, order)
    smem = pl.BlockSpec(memory_space=pltpu.SMEM)
    vmem = pl.BlockSpec(memory_space=pltpu.VMEM)
    block = (energies, 2, order, order)
    dma = pltpu.SemaphoreType.DMA
    return pl.pallas_call(
        functools.partial(kernel, n, slabs),
        out_shape=[jax.ShapeDtypeStruct(shape, F32)] * 2,
        in_specs=[smem, smem, smem, vmem, vmem, vmem],
        out_specs=[vmem, vmem],
        scratch_shapes=[
            pltpu.VMEM((9,) + block, F32),
            pltpu.VMEM((2, order, order), F32),
            pltpu.VMEM((4, order, order), BF16),
            pltpu.VMEM((4, order, order), BF16),
            pltpu.VMEM((4, order, order), BF16),
            pltpu.VMEM((4, order, order), BF16),
            pltpu.VMEM((2,) + block, F32),
            pltpu.VMEM((2,) + block, F32),
            pltpu.VMEM((2,) + block, F32),
            pltpu.VMEM(block, F32),
            pltpu.VMEM(block, F32),
            dma((3, energies)),
            dma((3, energies)),
            dma((2, CHUNKS)),
            dma((2, CHUNKS)),
            dma((2, CHUNKS)),
            dma((2, CHUNKS)),
            dma((2, CHUNKS)),
            dma((2, CHUNKS)),
        ],
        compiler_params=pltpu.CompilerParams(
            collective_id=0, has_side_effects=True, vmem_limit_bytes=60 * 2**20
        ),
    )(energy_real, energy_imag, table, jnp.stack([base, before]), coupling[0], deform[0])


def solution(mesh):
    return jax.shard_map(
        functools.partial(on_device, mesh.shape["energy"], mesh.shape["slab"]),
        mesh=mesh,
        in_specs=(
            P("energy"),
            P("energy"),
            P("slab", None),
            P("slab", None, None, None),
            P("slab", None, None, None),
            P("slab", None, None),
            P(),
            P(),
        ),
        out_specs=(P("energy", "slab", None, None, None), P("energy", "slab", None, None, None)),
        check_vma=False,
    )
```

```python
import functools

import jax
import jax.numpy as jnp
from jax import lax
from jax.experimental import pallas as pl
from jax.experimental.pallas import tpu as pltpu
from jax.sharding import PartitionSpec as P

MESH = pl.DeviceIdType.MESH
CHUNKS = 8
F32 = jnp.float32
BF16 = jnp.bfloat16


def split(value):
    high = value.astype(BF16)
    return high, (value - high.astype(F32)).astype(BF16)


def dot(left, right):
    return jnp.dot(left, right, preferred_element_type=F32)


def dot3(left, right):
    return dot(left[0], right[0]) + (dot(left[0], right[1]) + dot(left[1], right[0]))


def put_split(ref, place, value):
    ref[place], ref[place + 1] = split(value)


def get_split(ref, place):
    return ref[place], ref[place + 1]


def kernel(
    n, slabs, er_ref, ei_ref, table_ref, potential_ref, onsite_ref, coupling_ref, deform_ref,
    green_ref, sigma_ref,
    base_ref, big, couple, c_left, c_right, work, work2, pair, from_low, from_high, to_low, to_high,
    base_send, base_recv, slot_send, slot_recv, pair_send, pair_recv, low_send, low_recv, high_send, high_recv,
):
    energies = er_ref.shape[0]
    order = base_ref.shape[-1]
    rows = order // CHUNKS
    me = lax.axis_index("energy")
    q = lax.axis_index("slab")
    side = lax.rem(me, 2)
    partner = me + 1 - 2 * side
    has_low, has_high = me >= 2, me + 2 < n

    def at(energy, slab):
        return {"energy": energy, "slab": slab}

    barrier = pltpu.get_barrier_semaphore()

    def greet(present, energy, slab):
        @pl.when(present)
        def _():
            pl.semaphore_signal(barrier, inc=1, device_id=at(energy, slab), device_id_type=MESH)

    pl.semaphore_signal(barrier, inc=1, device_id=at(partner, q), device_id_type=MESH)
    greet(has_low, me - 2, q)
    greet(has_high, me + 2, q)
    greet(q >= 1, me, q - 1)
    greet(q + 1 < slabs, me, q + 1)

    identity_mask = lax.broadcasted_iota(jnp.int32, (order, order), 0) == lax.broadcasted_iota(
        jnp.int32, (order, order), 1
    )
    middle = max(slabs - 2, 1)
    base_ref[0, 0] = jnp.where(identity_mask, -potential_ref[...] - onsite_ref[0], -onsite_ref[0])
    base_ref[0, 1] = -onsite_ref[1]
    sigma_ref[...] = jnp.zeros_like(sigma_ref)
    for part in range(2):
        put_split(c_left, 2 * part, coupling_ref[part])
        put_split(c_right, 2 * part, coupling_ref[part].T)

    peers = 1
    for present in (has_low, has_high, q >= 1, q + 1 < slabs):
        peers = peers + jnp.where(present, 1, 0)
    pl.semaphore_wait(barrier, peers)

    base_copy = pltpu.make_async_remote_copy(
        src_ref=base_ref.at[0],
        dst_ref=base_ref.at[1],
        send_sem=base_send,
        recv_sem=base_recv,
        device_id=at(me, lax.rem(q + 1, slabs)),
        device_id_type=MESH,
    )

    @pl.when((q >= 1) & (q + 1 <= middle))
    def _():
        base_copy.start()

    @pl.when((q >= 2) & (q <= middle))
    def _():
        base_copy.wait_recv()

    def slot_copy(source, slot, energy):
        return pltpu.make_async_remote_copy(
            src_ref=big.at[source, energy],
            dst_ref=big.at[6 + slot, energy],
            send_sem=slot_send.at[slot, energy],
            recv_sem=slot_recv.at[slot, energy],
            device_id=at(me, lax.rem(q + 1, slabs)),
            device_id_type=MESH,
        )

    def compute(outer, sweep, energy):
        local = (outer == 0) & (sweep == 1) & (q >= 2)
        held = (outer == 1) & (sweep == 0)
        source = jnp.where(local, 0, 6 + outer * sweep)
        coupled = (q >= 1) & jnp.logical_not((outer == 0) & (sweep == 0))

        @pl.when(coupled & jnp.logical_not(local | held))
        def _():
            slot_copy(0, outer * sweep, energy).wait_recv()

        @pl.when(coupled)
        def _():
            put_split(work, 0, big[source, energy, 0])
            put_split(work, 2, big[source, energy, 1])
            cr, ci = get_split(c_left, 0), get_split(c_left, 2)
            gr, gi = get_split(work, 0), get_split(work, 2)
            tr = split(dot3(cr, gr) - dot3(ci, gi))
            ti = split(dot3(cr, gi) + dot3(ci, gr))
            dr, di = get_split(c_right, 0), get_split(c_right, 2)
            couple[0] = dot3(tr, dr) + dot3(ti, di)
            couple[1] = dot3(ti, dr) - dot3(tr, di)

        @pl.when(jnp.logical_not(coupled))
        def _():
            couple[...] = jnp.zeros_like(couple)

        which = jnp.where((outer == 0) & (sweep == 0), 1, 0)
        ar = base_ref[which, 0] - sigma_ref[energy, 0, 0] - couple[0]
        ai = base_ref[which, 1] - sigma_ref[energy, 0, 1] - couple[1]
        dr = jnp.where(identity_mask, ar + er_ref[energy], 0.0)
        di = jnp.where(identity_mask, ai + ei_ref[energy], 0.0)

        def reciprocal(axis):
            r, i = jnp.sum(dr, axis=axis, keepdims=True), jnp.sum(di, axis=axis, keepdims=True)
            modulus = r * r + i * i
            return r / modulus, -i / modulus

        col_r, col_i = reciprocal(0)
        row_r, row_i = reciprocal(1)
        off_r = jnp.where(identity_mask, 0.0, ar)
        off_i = jnp.where(identity_mask, 0.0, ai)
        w_r = off_r * col_r - off_i * col_i
        w_i = off_r * col_i + off_i * col_r
        couple[0], couple[1] = w_r, w_i
        put_split(work, 0, w_r)
        put_split(work, 2, w_i)
        wr, wi = get_split(work, 0), get_split(work, 2)
        s_r = dot3(wr, wr) - dot3(wi, wi)
        s_i = dot3(wr, wi) + dot3(wi, wr)
        put_split(work2, 0, s_r)
        put_split(work2, 2, s_i)
        sr, si = get_split(work2, 0), get_split(work2, 2)
        y_r = s_r - couple[0] - (dot3(wr, sr) - dot3(wi, si)) + jnp.where(identity_mask, 1.0, 0.0)
        y_i = s_i - couple[1] - (dot3(wr, si) + dot3(wi, sr))
        target = 3 * outer + sweep
        big[target, energy, 0] = row_r * y_r - row_i * y_i
        big[target, energy, 1] = row_r * y_i + row_i * y_r

        slot = jnp.where(outer == 0, 0, sweep + 1)
        first = (outer == 0) & (sweep == 1)
        second = (outer == 1) & (sweep == 0) & (q + 1 <= middle)
        third = (outer == 1) & (sweep == 1)

        @pl.when((q + 1 < slabs) & (first | second | third))
        def _():
            slot_copy(target, slot, energy).start()

    def pair_copy(outer, final, c):
        cut = pl.ds(c * rows, rows)
        return pltpu.make_async_remote_copy(
            src_ref=big.at[final, :, :, cut],
            dst_ref=pair.at[outer, :, :, cut],
            send_sem=pair_send.at[outer, c],
            recv_sem=pair_recv.at[outer, c],
            device_id=at(partner, q),
            device_id_type=MESH,
        )

    def low_copy(outer, c):
        cut = pl.ds(c * rows, rows)
        return pltpu.make_async_remote_copy(
            src_ref=to_low.at[:, :, cut],
            dst_ref=from_high.at[outer, :, :, cut],
            send_sem=low_send.at[outer, c],
            recv_sem=low_recv.at[outer, c],
            device_id=at(lax.rem(me + n - 2, n), q),
            device_id_type=MESH,
        )

    def high_copy(outer, c):
        cut = pl.ds(c * rows, rows)
        return pltpu.make_async_remote_copy(
            src_ref=to_high.at[:, :, cut],
            dst_ref=from_low.at[outer, :, :, cut],
            send_sem=high_send.at[outer, c],
            recv_sem=high_recv.at[outer, c],
            device_id=at(lax.rem(me + 2, n), q),
            device_id_type=MESH,
        )

    zero_at = 4 * energies - 1
    step_to_partner = energies * (1 - 2 * side)
    strip = 8

    def each_strip(c, body):
        def one(index, carry):
            body(pl.ds(pl.multiple_of(c * rows + index * strip, strip), strip))
            return carry

        lax.fori_loop(0, rows // strip, one, 0)

    def exchange(outer):
        final = jnp.where(outer == 0, jnp.where(q >= 2, 2, 1), 3 + jnp.minimum(q, 2))
        for c in range(CHUNKS):
            pair_copy(outer, final, c).start()
        for c in range(CHUNKS):
            pair_copy(outer, final, c).wait_recv()

            def sums(shift, goal, final=final):
                weight = [
                    [
                        [
                            table_ref[zero_at + shift + b - a + extra]
                            for extra in (0, step_to_partner)
                        ]
                        for b in range(energies)
                    ]
                    for a in range(energies)
                ]

                def body(cut):
                    for part in range(2):
                        own = [big[final, b, part, cut] for b in range(energies)]
                        other = [pair[outer, b, part, cut] for b in range(energies)]
                        for a in range(energies):
                            total = weight[a][0][0] * own[0]
                            for b in range(energies):
                                if b:
                                    total = total + weight[a][b][0] * own[b]
                                total = total + weight[a][b][1] * other[b]
                            goal(a, part, cut, total)

                each_strip(c, body)

            def put_high(a, part, cut, value):
                to_high[a, part, cut] = value

            def put_low(a, part, cut, value):
                to_low[a, part, cut] = value

            def put_own(a, part, cut, value):
                sigma_ref[a, 0, part, cut] = value

            @pl.when(has_high)
            def _():
                sums(-2 * energies, put_high)
                high_copy(outer, c).start()

            @pl.when(has_low)
            def _():
                sums(2 * energies, put_low)
                low_copy(outer, c).start()

            sums(0, put_own)

        for c in range(CHUNKS):

            def add(source):
                def body(cut):
                    for a in range(energies):
                        for part in range(2):
                            sigma_ref[a, 0, part, cut] += source[outer, a, part, cut]

                each_strip(c, body)

            @pl.when(has_low)
            def _():
                high_copy(outer, c).wait_recv()
                add(from_low)

            @pl.when(has_high)
            def _():
                low_copy(outer, c).wait_recv()
                add(from_high)

            def scale(cut):
                level = deform_ref[cut]
                for a in range(energies):
                    for part in range(2):
                        sigma_ref[a, 0, part, cut] = level * sigma_ref[a, 0, part, cut]

            each_strip(c, scale)

        for c in range(CHUNKS):
            pair_copy(outer, final, c).wait_send()

            @pl.when(has_high)
            def _():
                high_copy(outer, c).wait_send()

            @pl.when(has_low)
            def _():
                low_copy(outer, c).wait_send()

    def outer_step(outer, carry):
        def step(j, inner):
            paired = (outer == 0) & (j < 2 * energies)
            sweep = jnp.where(paired, lax.rem(j, 2), lax.div(j, energies))
            energy = jnp.where(paired, lax.div(j, 2), lax.rem(j, energies))
            start = ((outer == 0) & (q >= 2) & (q <= middle)) | ((outer == 1) & (q <= 1))
            mid = (q <= middle) & ((outer == 0) | (q >= 1))
            active = (
                ((sweep == 0) & start) | ((sweep == 1) & mid) | ((sweep == 2) & (q >= 2))
            )

            @pl.when(active)
            def _():
                compute(outer, sweep, energy)

            return inner

        lax.fori_loop(0, 3 * energies, step, 0)
        exchange(outer)
        return carry

    lax.fori_loop(0, 2, outer_step, 0)

    final = 3 + jnp.minimum(q, 2)

    def out(index, carry):
        cut = pl.ds(pl.multiple_of(index * 64, 64), 64)
        for a in range(energies):
            for part in range(2):
                green_ref[a, 0, part, cut] = big[final, a, part, cut]
        return carry

    lax.fori_loop(0, order // 64, out, 0)

    def drain(slot, present):
        @pl.when(present & (q + 1 < slabs))
        def _():
            for energy in range(energies):
                slot_copy(0, slot, energy).wait_send()

    drain(0, q <= middle)
    drain(1, q + 1 <= middle)
    drain(2, (q >= 1) & (q <= middle))

    @pl.when((q >= 1) & (q + 1 <= middle))
    def _():
        base_copy.wait_send()


def on_device(n, slabs, energy_real, energy_imag, potential, onsite, coupling, deform, offsets, weights):
    order = onsite.shape[-1]
    energies = energy_real.shape[0]
    gap = jnp.arange(8 * energies - 1, dtype=jnp.int32) - (4 * energies - 1)
    table = jnp.sum(
        jnp.where(gap[:, None] == offsets[None, :], weights.astype(F32)[None, :] / 128.0, 0.0), axis=-1
    )
    shape = (energies, 1, 2, order, order)
    smem = pl.BlockSpec(memory_space=pltpu.SMEM)
    vmem = pl.BlockSpec(memory_space=pltpu.VMEM)
    block = (energies, 2, order, order)
    dma = pltpu.SemaphoreType.DMA
    return pl.pallas_call(
        functools.partial(kernel, n, slabs),
        out_shape=[jax.ShapeDtypeStruct(shape, F32)] * 2,
        in_specs=[smem, smem, smem, vmem, vmem, vmem, vmem],
        out_specs=[vmem, vmem],
        scratch_shapes=[
            pltpu.VMEM((2, 2, order, order), F32),
            pltpu.VMEM((9,) + block, F32),
            pltpu.VMEM((2, order, order), F32),
            pltpu.VMEM((4, order, order), BF16),
            pltpu.VMEM((4, order, order), BF16),
            pltpu.VMEM((4, order, order), BF16),
            pltpu.VMEM((4, order, order), BF16),
            pltpu.VMEM((2,) + block, F32),
            pltpu.VMEM((2,) + block, F32),
            pltpu.VMEM((2,) + block, F32),
            pltpu.VMEM(block, F32),
            pltpu.VMEM(block, F32),
            dma,
            dma,
            dma((3, energies)),
            dma((3, energies)),
            dma((2, CHUNKS)),
            dma((2, CHUNKS)),
            dma((2, CHUNKS)),
            dma((2, CHUNKS)),
            dma((2, CHUNKS)),
            dma((2, CHUNKS)),
        ],
        compiler_params=pltpu.CompilerParams(
            collective_id=0, has_side_effects=True, vmem_limit_bytes=60 * 2**20
        ),
    )(energy_real, energy_imag, table, potential, onsite[0], coupling[0], deform[0])


def solution(mesh):
    return jax.shard_map(
        functools.partial(on_device, mesh.shape["energy"], mesh.shape["slab"]),
        mesh=mesh,
        in_specs=(
            P("energy"),
            P("energy"),
            P("slab", None),
            P("slab", None, None, None),
            P("slab", None, None, None),
            P("slab", None, None),
            P(),
            P(),
        ),
        out_specs=(P("energy", "slab", None, None, None), P("energy", "slab", None, None, None)),
        check_vma=False,
    )
```

```python
import functools

import jax
import jax.numpy as jnp
from jax import lax
from jax.experimental import pallas as pl
from jax.experimental.pallas import tpu as pltpu
from jax.sharding import PartitionSpec as P

MESH = pl.DeviceIdType.MESH
CHUNKS = 8
AHEAD = 3
F32 = jnp.float32
BF16 = jnp.bfloat16


def split(value):
    high = value.astype(BF16)
    return high, (value - high.astype(F32)).astype(BF16)


def dot(left, right):
    return jnp.dot(left, right, preferred_element_type=F32)


def dot3(left, right):
    return dot(left[0], right[0]) + (dot(left[0], right[1]) + dot(left[1], right[0]))


def put_split(ref, place, value):
    ref[place], ref[place + 1] = split(value)


def get_split(ref, place):
    return ref[place], ref[place + 1]


def kernel(
    n, slabs, er_ref, ei_ref, table_ref, potential_ref, onsite_ref, coupling_ref, deform_ref,
    green_ref, sigma_ref,
    base_ref, big, couple, c_left, c_right, work, work2, pair, from_low, from_high, to_low, to_high,
    go, base_send, base_recv, slot_send, slot_recv, pair_send, pair_recv, low_send, low_recv, high_send, high_recv,
):
    energies = er_ref.shape[0]
    order = base_ref.shape[-1]
    rows = order // CHUNKS
    me = lax.axis_index("energy")
    q = lax.axis_index("slab")
    side = lax.rem(me, 2)
    partner = me + 1 - 2 * side
    has_low, has_high = me >= 2, me + 2 < n

    def at(energy, slab):
        return {"energy": energy, "slab": slab}

    barrier = pltpu.get_barrier_semaphore()

    def greet(present, energy, slab):
        @pl.when(present)
        def _():
            pl.semaphore_signal(barrier, inc=1, device_id=at(energy, slab), device_id_type=MESH)

    pl.semaphore_signal(barrier, inc=1, device_id=at(partner, q), device_id_type=MESH)
    greet(has_low, me - 2, q)
    greet(has_high, me + 2, q)
    greet(q >= 1, me, q - 1)
    greet(q + 1 < slabs, me, q + 1)

    identity_mask = lax.broadcasted_iota(jnp.int32, (order, order), 0) == lax.broadcasted_iota(
        jnp.int32, (order, order), 1
    )
    middle = max(slabs - 2, 1)
    base_ref[0, 0] = jnp.where(identity_mask, -potential_ref[...] - onsite_ref[0], -onsite_ref[0])
    base_ref[0, 1] = -onsite_ref[1]
    sigma_ref[...] = jnp.zeros_like(sigma_ref)
    for part in range(2):
        put_split(c_left, 2 * part, coupling_ref[part])
        put_split(c_right, 2 * part, coupling_ref[part].T)

    peers = 1
    for present in (has_low, has_high, q >= 1, q + 1 < slabs):
        peers = peers + jnp.where(present, 1, 0)
    pl.semaphore_wait(barrier, peers)

    base_copy = pltpu.make_async_remote_copy(
        src_ref=base_ref.at[0],
        dst_ref=base_ref.at[1],
        send_sem=base_send,
        recv_sem=base_recv,
        device_id=at(me, lax.rem(q + 1, slabs)),
        device_id_type=MESH,
    )

    @pl.when((q >= 1) & (q + 1 <= middle))
    def _():
        base_copy.start()

    @pl.when((q >= 2) & (q <= middle))
    def _():
        base_copy.wait_recv()

    def slot_copy(source, slot, energy):
        return pltpu.make_async_remote_copy(
            src_ref=big.at[source, energy],
            dst_ref=big.at[6 + slot, energy],
            send_sem=slot_send.at[slot, energy],
            recv_sem=slot_recv.at[slot, energy],
            device_id=at(me, lax.rem(q + 1, slabs)),
            device_id_type=MESH,
        )

    def compute(outer, sweep, energy):
        local = (outer == 0) & (sweep == 1) & (q >= 2)
        held = (outer == 1) & (sweep == 0)
        source = jnp.where(local, 0, 6 + outer * sweep)
        coupled = (q >= 1) & jnp.logical_not((outer == 0) & (sweep == 0))

        @pl.when(coupled & jnp.logical_not(local | held))
        def _():
            slot_copy(0, outer * sweep, energy).wait_recv()

        @pl.when(coupled)
        def _():
            put_split(work, 0, big[source, energy, 0])
            put_split(work, 2, big[source, energy, 1])
            cr, ci = get_split(c_left, 0), get_split(c_left, 2)
            gr, gi = get_split(work, 0), get_split(work, 2)
            tr = split(dot3(cr, gr) - dot3(ci, gi))
            ti = split(dot3(cr, gi) + dot3(ci, gr))
            dr, di = get_split(c_right, 0), get_split(c_right, 2)
            couple[0] = dot3(tr, dr) + dot3(ti, di)
            couple[1] = dot3(ti, dr) - dot3(tr, di)

        @pl.when(jnp.logical_not(coupled))
        def _():
            couple[...] = jnp.zeros_like(couple)

        which = jnp.where((outer == 0) & (sweep == 0), 1, 0)
        ar = base_ref[which, 0] - sigma_ref[energy, 0, 0] - couple[0]
        ai = base_ref[which, 1] - sigma_ref[energy, 0, 1] - couple[1]
        dr = jnp.where(identity_mask, ar + er_ref[energy], 0.0)
        di = jnp.where(identity_mask, ai + ei_ref[energy], 0.0)

        def reciprocal(axis):
            r, i = jnp.sum(dr, axis=axis, keepdims=True), jnp.sum(di, axis=axis, keepdims=True)
            modulus = r * r + i * i
            return r / modulus, -i / modulus

        col_r, col_i = reciprocal(0)
        row_r, row_i = reciprocal(1)
        off_r = jnp.where(identity_mask, 0.0, ar)
        off_i = jnp.where(identity_mask, 0.0, ai)
        w_r = off_r * col_r - off_i * col_i
        w_i = off_r * col_i + off_i * col_r
        couple[0], couple[1] = w_r, w_i
        put_split(work, 0, w_r)
        put_split(work, 2, w_i)
        wr, wi = get_split(work, 0), get_split(work, 2)
        s_r = dot3(wr, wr) - dot3(wi, wi)
        s_i = dot3(wr, wi) + dot3(wi, wr)
        put_split(work2, 0, s_r)
        put_split(work2, 2, s_i)
        sr, si = get_split(work2, 0), get_split(work2, 2)
        y_r = s_r - couple[0] - (dot3(wr, sr) - dot3(wi, si)) + jnp.where(identity_mask, 1.0, 0.0)
        y_i = s_i - couple[1] - (dot3(wr, si) + dot3(wi, sr))
        target = 3 * outer + sweep
        big[target, energy, 0] = row_r * y_r - row_i * y_i
        big[target, energy, 1] = row_r * y_i + row_i * y_r

        slot = jnp.where(outer == 0, 0, sweep + 1)
        first = (outer == 0) & (sweep == 1)
        second = (outer == 1) & (sweep == 0) & (q + 1 <= middle)
        third = (outer == 1) & (sweep == 1)

        @pl.when((q + 1 < slabs) & (first | second | third))
        def _():
            slot_copy(target, slot, energy).start()

    def pair_copy(outer, final, c):
        cut = pl.ds(c * rows, rows)
        return pltpu.make_async_remote_copy(
            src_ref=big.at[final, :, :, cut],
            dst_ref=pair.at[outer, :, :, cut],
            send_sem=pair_send.at[outer, c],
            recv_sem=pair_recv.at[outer, c],
            device_id=at(partner, q),
            device_id_type=MESH,
        )

    def low_copy(outer, c):
        cut = pl.ds(c * rows, rows)
        return pltpu.make_async_remote_copy(
            src_ref=to_low.at[:, :, cut],
            dst_ref=from_high.at[outer, :, :, cut],
            send_sem=low_send.at[outer, c],
            recv_sem=low_recv.at[outer, c],
            device_id=at(lax.rem(me + n - 2, n), q),
            device_id_type=MESH,
        )

    def high_copy(outer, c):
        cut = pl.ds(c * rows, rows)
        return pltpu.make_async_remote_copy(
            src_ref=to_high.at[:, :, cut],
            dst_ref=from_low.at[outer, :, :, cut],
            send_sem=high_send.at[outer, c],
            recv_sem=high_recv.at[outer, c],
            device_id=at(lax.rem(me + 2, n), q),
            device_id_type=MESH,
        )

    zero_at = 4 * energies - 1
    step_to_partner = energies * (1 - 2 * side)
    strip = 8

    def each_strip(c, body):
        def one(index, carry):
            body(pl.ds(pl.multiple_of(c * rows + index * strip, strip), strip))
            return carry

        lax.fori_loop(0, rows // strip, one, 0)

    def exchange(outer):
        final = jnp.where(outer == 0, jnp.where(q >= 2, 2, 1), 3 + jnp.minimum(q, 2))
        yields = (outer == 0) & (q == 0) & (slabs >= 2)

        def start_rest():
            for c in range(AHEAD, CHUNKS):
                pair_copy(outer, final, c).start()

        for c in range(AHEAD):
            pair_copy(outer, final, c).start()
        pl.when(jnp.logical_not(yields))(start_rest)
        for c in range(CHUNKS):
            if c == AHEAD:

                @pl.when(yields)
                def _():
                    pl.semaphore_wait(go, 1)
                    start_rest()

            pair_copy(outer, final, c).wait_recv()
            if c == CHUNKS - 2:

                @pl.when((outer == 0) & (q == 1))
                def _():
                    pl.semaphore_signal(go, inc=1, device_id=at(me, q - 1), device_id_type=MESH)

            def sums(shift, goal, final=final):
                weight = [
                    [
                        [
                            table_ref[zero_at + shift + b - a + extra]
                            for extra in (0, step_to_partner)
                        ]
                        for b in range(energies)
                    ]
                    for a in range(energies)
                ]

                def body(cut):
                    for part in range(2):
                        own = [big[final, b, part, cut] for b in range(energies)]
                        other = [pair[outer, b, part, cut] for b in range(energies)]
                        for a in range(energies):
                            total = weight[a][0][0] * own[0]
                            for b in range(energies):
                                if b:
                                    total = total + weight[a][b][0] * own[b]
                                total = total + weight[a][b][1] * other[b]
                            goal(a, part, cut, total)

                each_strip(c, body)

            def put_high(a, part, cut, value):
                to_high[a, part, cut] = value

            def put_low(a, part, cut, value):
                to_low[a, part, cut] = value

            def put_own(a, part, cut, value):
                sigma_ref[a, 0, part, cut] = value

            @pl.when(has_high)
            def _():
                sums(-2 * energies, put_high)
                high_copy(outer, c).start()

            @pl.when(has_low)
            def _():
                sums(2 * energies, put_low)
                low_copy(outer, c).start()

            sums(0, put_own)

        for c in range(CHUNKS):

            def add(source):
                def body(cut):
                    for a in range(energies):
                        for part in range(2):
                            sigma_ref[a, 0, part, cut] += source[outer, a, part, cut]

                each_strip(c, body)

            @pl.when(has_low)
            def _():
                high_copy(outer, c).wait_recv()
                add(from_low)

            @pl.when(has_high)
            def _():
                low_copy(outer, c).wait_recv()
                add(from_high)

            def scale(cut):
                level = deform_ref[cut]
                for a in range(energies):
                    for part in range(2):
                        sigma_ref[a, 0, part, cut] = level * sigma_ref[a, 0, part, cut]

            each_strip(c, scale)

        for c in range(CHUNKS):
            pair_copy(outer, final, c).wait_send()

            @pl.when(has_high)
            def _():
                high_copy(outer, c).wait_send()

            @pl.when(has_low)
            def _():
                low_copy(outer, c).wait_send()

    def outer_step(outer, carry):
        def step(j, inner):
            paired = (outer == 0) & (j < 2 * energies)
            sweep = jnp.where(paired, lax.rem(j, 2), lax.div(j, energies))
            energy = jnp.where(paired, lax.div(j, 2), lax.rem(j, energies))
            start = ((outer == 0) & (q >= 2) & (q <= middle)) | ((outer == 1) & (q <= 1))
            mid = (q <= middle) & ((outer == 0) | (q >= 1))
            active = (
                ((sweep == 0) & start) | ((sweep == 1) & mid) | ((sweep == 2) & (q >= 2))
            )

            @pl.when(active)
            def _():
                compute(outer, sweep, energy)

            return inner

        lax.fori_loop(0, 3 * energies, step, 0)
        exchange(outer)
        return carry

    lax.fori_loop(0, 2, outer_step, 0)

    final = 3 + jnp.minimum(q, 2)

    def out(index, carry):
        cut = pl.ds(pl.multiple_of(index * 64, 64), 64)
        for a in range(energies):
            for part in range(2):
                green_ref[a, 0, part, cut] = big[final, a, part, cut]
        return carry

    lax.fori_loop(0, order // 64, out, 0)

    def drain(slot, present):
        @pl.when(present & (q + 1 < slabs))
        def _():
            for energy in range(energies):
                slot_copy(0, slot, energy).wait_send()

    drain(0, q <= middle)
    drain(1, q + 1 <= middle)
    drain(2, (q >= 1) & (q <= middle))

    @pl.when((q >= 1) & (q + 1 <= middle))
    def _():
        base_copy.wait_send()


def on_device(n, slabs, energy_real, energy_imag, potential, onsite, coupling, deform, offsets, weights):
    order = onsite.shape[-1]
    energies = energy_real.shape[0]
    gap = jnp.arange(8 * energies - 1, dtype=jnp.int32) - (4 * energies - 1)
    table = jnp.sum(
        jnp.where(gap[:, None] == offsets[None, :], weights.astype(F32)[None, :] / 128.0, 0.0), axis=-1
    )
    shape = (energies, 1, 2, order, order)
    smem = pl.BlockSpec(memory_space=pltpu.SMEM)
    vmem = pl.BlockSpec(memory_space=pltpu.VMEM)
    block = (energies, 2, order, order)
    dma = pltpu.SemaphoreType.DMA
    return pl.pallas_call(
        functools.partial(kernel, n, slabs),
        out_shape=[jax.ShapeDtypeStruct(shape, F32)] * 2,
        in_specs=[smem, smem, smem, vmem, vmem, vmem, vmem],
        out_specs=[vmem, vmem],
        scratch_shapes=[
            pltpu.VMEM((2, 2, order, order), F32),
            pltpu.VMEM((9,) + block, F32),
            pltpu.VMEM((2, order, order), F32),
            pltpu.VMEM((4, order, order), BF16),
            pltpu.VMEM((4, order, order), BF16),
            pltpu.VMEM((4, order, order), BF16),
            pltpu.VMEM((4, order, order), BF16),
            pltpu.VMEM((2,) + block, F32),
            pltpu.VMEM((2,) + block, F32),
            pltpu.VMEM((2,) + block, F32),
            pltpu.VMEM(block, F32),
            pltpu.VMEM(block, F32),
            pltpu.SemaphoreType.REGULAR,
            dma,
            dma,
            dma((3, energies)),
            dma((3, energies)),
            dma((2, CHUNKS)),
            dma((2, CHUNKS)),
            dma((2, CHUNKS)),
            dma((2, CHUNKS)),
            dma((2, CHUNKS)),
            dma((2, CHUNKS)),
        ],
        compiler_params=pltpu.CompilerParams(
            collective_id=0, has_side_effects=True, vmem_limit_bytes=60 * 2**20
        ),
    )(energy_real, energy_imag, table, potential, onsite[0], coupling[0], deform[0])


def solution(mesh):
    return jax.shard_map(
        functools.partial(on_device, mesh.shape["energy"], mesh.shape["slab"]),
        mesh=mesh,
        in_specs=(
            P("energy"),
            P("energy"),
            P("slab", None),
            P("slab", None, None, None),
            P("slab", None, None, None),
            P("slab", None, None),
            P(),
            P(),
        ),
        out_specs=(P("energy", "slab", None, None, None), P("energy", "slab", None, None, None)),
        check_vma=False,
    )
```

```python
import functools

import jax
import jax.numpy as jnp
from jax import lax
from jax.experimental import pallas as pl
from jax.experimental.pallas import tpu as pltpu
from jax.sharding import PartitionSpec as P

MESH = pl.DeviceIdType.MESH
CHUNKS = 8
AHEAD = 3
F32 = jnp.float32
BF16 = jnp.bfloat16


def split(value):
    high = value.astype(BF16)
    return high, (value - high.astype(F32)).astype(BF16)


def put_left(ref, real, imag):
    order = real.shape[0]
    real_high, real_low = split(real)
    imag_high, imag_low = split(imag)
    top = (-imag_high, -imag_high, -imag_low, real_high, real_high, real_low)
    bottom = (real_high, real_high, real_low, imag_high, imag_high, imag_low)
    for place in range(6):
        cut = slice(place * order, (place + 1) * order)
        ref[:order, cut] = top[place]
        ref[order:, cut] = bottom[place]


def put_right(ref, real, imag):
    order = real.shape[0]
    real_high, real_low = split(real)
    imag_high, imag_low = split(imag)
    parts = (imag_high, imag_low, imag_high, real_high, real_low, real_high)
    for place in range(6):
        ref[place * order : (place + 1) * order] = parts[place]


def product(left, right):
    both = jnp.dot(left[...], right[...], preferred_element_type=F32)
    order = right.shape[1]
    return both[:order], both[order:]


def kernel(
    n, slabs, er_ref, ei_ref, table_ref, potential_ref, onsite_ref, coupling_ref, deform_ref,
    green_ref, sigma_ref,
    base_ref, big, couple, c_left, c_right, left, right, pair, from_low, from_high, to_low, to_high,
    go, base_send, base_recv, slot_send, slot_recv, pair_send, pair_recv, low_send, low_recv, high_send, high_recv,
):
    energies = er_ref.shape[0]
    order = base_ref.shape[-1]
    rows = order // CHUNKS
    me = lax.axis_index("energy")
    q = lax.axis_index("slab")
    side = lax.rem(me, 2)
    partner = me + 1 - 2 * side
    has_low, has_high = me >= 2, me + 2 < n

    def at(energy, slab):
        return {"energy": energy, "slab": slab}

    barrier = pltpu.get_barrier_semaphore()

    def greet(present, energy, slab):
        @pl.when(present)
        def _():
            pl.semaphore_signal(barrier, inc=1, device_id=at(energy, slab), device_id_type=MESH)

    pl.semaphore_signal(barrier, inc=1, device_id=at(partner, q), device_id_type=MESH)
    greet(has_low, me - 2, q)
    greet(has_high, me + 2, q)
    greet(q >= 1, me, q - 1)
    greet(q + 1 < slabs, me, q + 1)

    identity_mask = lax.broadcasted_iota(jnp.int32, (order, order), 0) == lax.broadcasted_iota(
        jnp.int32, (order, order), 1
    )
    middle = max(slabs - 2, 1)
    base_ref[0, 0] = jnp.where(identity_mask, -potential_ref[...] - onsite_ref[0], -onsite_ref[0])
    base_ref[0, 1] = -onsite_ref[1]
    sigma_ref[...] = jnp.zeros_like(sigma_ref)
    put_left(c_left, coupling_ref[0], coupling_ref[1])
    put_right(c_right, coupling_ref[0].T, -coupling_ref[1].T)

    peers = 1
    for present in (has_low, has_high, q >= 1, q + 1 < slabs):
        peers = peers + jnp.where(present, 1, 0)
    pl.semaphore_wait(barrier, peers)

    base_copy = pltpu.make_async_remote_copy(
        src_ref=base_ref.at[0],
        dst_ref=base_ref.at[1],
        send_sem=base_send,
        recv_sem=base_recv,
        device_id=at(me, lax.rem(q + 1, slabs)),
        device_id_type=MESH,
    )

    @pl.when((q >= 1) & (q + 1 <= middle))
    def _():
        base_copy.start()

    @pl.when((q >= 2) & (q <= middle))
    def _():
        base_copy.wait_recv()

    def slot_copy(source, slot, energy):
        return pltpu.make_async_remote_copy(
            src_ref=big.at[source, energy],
            dst_ref=big.at[6 + slot, energy],
            send_sem=slot_send.at[slot, energy],
            recv_sem=slot_recv.at[slot, energy],
            device_id=at(me, lax.rem(q + 1, slabs)),
            device_id_type=MESH,
        )

    def compute(outer, sweep, energy):
        local = (outer == 0) & (sweep == 1) & (q >= 2)
        held = (outer == 1) & (sweep == 0)
        source = jnp.where(local, 0, 6 + outer * sweep)
        coupled = (q >= 1) & jnp.logical_not((outer == 0) & (sweep == 0))

        @pl.when(coupled & jnp.logical_not(local | held))
        def _():
            slot_copy(0, outer * sweep, energy).wait_recv()

        @pl.when(coupled)
        def _():
            put_right(right, big[source, energy, 0], big[source, energy, 1])
            put_left(left, *product(c_left, right))
            couple[0], couple[1] = product(left, c_right)

        @pl.when(jnp.logical_not(coupled))
        def _():
            couple[...] = jnp.zeros_like(couple)

        which = jnp.where((outer == 0) & (sweep == 0), 1, 0)
        ar = base_ref[which, 0] - sigma_ref[energy, 0, 0] - couple[0]
        ai = base_ref[which, 1] - sigma_ref[energy, 0, 1] - couple[1]
        dr = jnp.where(identity_mask, ar + er_ref[energy], 0.0)
        di = jnp.where(identity_mask, ai + ei_ref[energy], 0.0)

        def reciprocal(axis):
            r, i = jnp.sum(dr, axis=axis, keepdims=True), jnp.sum(di, axis=axis, keepdims=True)
            modulus = r * r + i * i
            return r / modulus, -i / modulus

        col_r, col_i = reciprocal(0)
        row_r, row_i = reciprocal(1)
        off_r = jnp.where(identity_mask, 0.0, ar)
        off_i = jnp.where(identity_mask, 0.0, ai)
        w_r = off_r * col_r - off_i * col_i
        w_i = off_r * col_i + off_i * col_r
        couple[0], couple[1] = w_r, w_i
        put_left(left, w_r, w_i)
        put_right(right, w_r, w_i)
        s_r, s_i = product(left, right)
        couple[0] = s_r - couple[0] + jnp.where(identity_mask, 1.0, 0.0)
        couple[1] = s_i - couple[1]
        put_right(right, s_r, s_i)
        p_r, p_i = product(left, right)
        y_r, y_i = couple[0] - p_r, couple[1] - p_i
        target = 3 * outer + sweep
        big[target, energy, 0] = row_r * y_r - row_i * y_i
        big[target, energy, 1] = row_r * y_i + row_i * y_r

        slot = jnp.where(outer == 0, 0, sweep + 1)
        first = (outer == 0) & (sweep == 1)
        second = (outer == 1) & (sweep == 0) & (q + 1 <= middle)
        third = (outer == 1) & (sweep == 1)

        @pl.when((q + 1 < slabs) & (first | second | third))
        def _():
            slot_copy(target, slot, energy).start()

    def pair_copy(outer, final, c):
        cut = pl.ds(c * rows, rows)
        return pltpu.make_async_remote_copy(
            src_ref=big.at[final, :, :, cut],
            dst_ref=pair.at[outer, :, :, cut],
            send_sem=pair_send.at[outer, c],
            recv_sem=pair_recv.at[outer, c],
            device_id=at(partner, q),
            device_id_type=MESH,
        )

    def low_copy(outer, c):
        cut = pl.ds(c * rows, rows)
        return pltpu.make_async_remote_copy(
            src_ref=to_low.at[:, :, cut],
            dst_ref=from_high.at[outer, :, :, cut],
            send_sem=low_send.at[outer, c],
            recv_sem=low_recv.at[outer, c],
            device_id=at(lax.rem(me + n - 2, n), q),
            device_id_type=MESH,
        )

    def high_copy(outer, c):
        cut = pl.ds(c * rows, rows)
        return pltpu.make_async_remote_copy(
            src_ref=to_high.at[:, :, cut],
            dst_ref=from_low.at[outer, :, :, cut],
            send_sem=high_send.at[outer, c],
            recv_sem=high_recv.at[outer, c],
            device_id=at(lax.rem(me + 2, n), q),
            device_id_type=MESH,
        )

    zero_at = 4 * energies - 1
    step_to_partner = energies * (1 - 2 * side)
    strip = 8

    def each_strip(c, body):
        def one(index, carry):
            body(pl.ds(pl.multiple_of(c * rows + index * strip, strip), strip))
            return carry

        lax.fori_loop(0, rows // strip, one, 0)

    def exchange(outer):
        final = jnp.where(outer == 0, jnp.where(q >= 2, 2, 1), 3 + jnp.minimum(q, 2))
        yields = (outer == 0) & (q == 0) & (slabs >= 2)

        def start_rest():
            for c in range(AHEAD, CHUNKS):
                pair_copy(outer, final, c).start()

        for c in range(AHEAD):
            pair_copy(outer, final, c).start()
        pl.when(jnp.logical_not(yields))(start_rest)
        for c in range(CHUNKS):
            if c == AHEAD:

                @pl.when(yields)
                def _():
                    pl.semaphore_wait(go, 1)
                    start_rest()

            pair_copy(outer, final, c).wait_recv()
            if c == CHUNKS - 2:

                @pl.when((outer == 0) & (q == 1))
                def _():
                    pl.semaphore_signal(go, inc=1, device_id=at(me, q - 1), device_id_type=MESH)

            def sums(shift, goal, final=final):
                weight = [
                    [
                        [
                            table_ref[zero_at + shift + b - a + extra]
                            for extra in (0, step_to_partner)
                        ]
                        for b in range(energies)
                    ]
                    for a in range(energies)
                ]

                def body(cut):
                    for part in range(2):
                        own = [big[final, b, part, cut] for b in range(energies)]
                        other = [pair[outer, b, part, cut] for b in range(energies)]
                        for a in range(energies):
                            total = weight[a][0][0] * own[0]
                            for b in range(energies):
                                if b:
                                    total = total + weight[a][b][0] * own[b]
                                total = total + weight[a][b][1] * other[b]
                            goal(a, part, cut, total)

                each_strip(c, body)

            def put_high(a, part, cut, value):
                to_high[a, part, cut] = value

            def put_low(a, part, cut, value):
                to_low[a, part, cut] = value

            def put_own(a, part, cut, value):
                sigma_ref[a, 0, part, cut] = value

            @pl.when(has_high)
            def _():
                sums(-2 * energies, put_high)
                high_copy(outer, c).start()

            @pl.when(has_low)
            def _():
                sums(2 * energies, put_low)
                low_copy(outer, c).start()

            sums(0, put_own)

        for c in range(CHUNKS):

            def add(source):
                def body(cut):
                    for a in range(energies):
                        for part in range(2):
                            sigma_ref[a, 0, part, cut] += source[outer, a, part, cut]

                each_strip(c, body)

            @pl.when(has_low)
            def _():
                high_copy(outer, c).wait_recv()
                add(from_low)

            @pl.when(has_high)
            def _():
                low_copy(outer, c).wait_recv()
                add(from_high)

            def scale(cut):
                level = deform_ref[cut]
                for a in range(energies):
                    for part in range(2):
                        sigma_ref[a, 0, part, cut] = level * sigma_ref[a, 0, part, cut]

            each_strip(c, scale)

        for c in range(CHUNKS):
            pair_copy(outer, final, c).wait_send()

            @pl.when(has_high)
            def _():
                high_copy(outer, c).wait_send()

            @pl.when(has_low)
            def _():
                low_copy(outer, c).wait_send()

    def outer_step(outer, carry):
        def step(j, inner):
            paired = (outer == 0) & (j < 2 * energies)
            sweep = jnp.where(paired, lax.rem(j, 2), lax.div(j, energies))
            energy = jnp.where(paired, lax.div(j, 2), lax.rem(j, energies))
            start = ((outer == 0) & (q >= 2) & (q <= middle)) | ((outer == 1) & (q <= 1))
            mid = (q <= middle) & ((outer == 0) | (q >= 1))
            active = (
                ((sweep == 0) & start) | ((sweep == 1) & mid) | ((sweep == 2) & (q >= 2))
            )

            @pl.when(active)
            def _():
                compute(outer, sweep, energy)

            return inner

        lax.fori_loop(0, 3 * energies, step, 0)
        exchange(outer)
        return carry

    lax.fori_loop(0, 2, outer_step, 0)

    final = 3 + jnp.minimum(q, 2)

    def out(index, carry):
        cut = pl.ds(pl.multiple_of(index * 64, 64), 64)
        for a in range(energies):
            for part in range(2):
                green_ref[a, 0, part, cut] = big[final, a, part, cut]
        return carry

    lax.fori_loop(0, order // 64, out, 0)

    def drain(slot, present):
        @pl.when(present & (q + 1 < slabs))
        def _():
            for energy in range(energies):
                slot_copy(0, slot, energy).wait_send()

    drain(0, q <= middle)
    drain(1, q + 1 <= middle)
    drain(2, (q >= 1) & (q <= middle))

    @pl.when((q >= 1) & (q + 1 <= middle))
    def _():
        base_copy.wait_send()


def on_device(n, slabs, energy_real, energy_imag, potential, onsite, coupling, deform, offsets, weights):
    order = onsite.shape[-1]
    energies = energy_real.shape[0]
    gap = jnp.arange(8 * energies - 1, dtype=jnp.int32) - (4 * energies - 1)
    table = jnp.sum(
        jnp.where(gap[:, None] == offsets[None, :], weights.astype(F32)[None, :] / 128.0, 0.0), axis=-1
    )
    shape = (energies, 1, 2, order, order)
    smem = pl.BlockSpec(memory_space=pltpu.SMEM)
    vmem = pl.BlockSpec(memory_space=pltpu.VMEM)
    block = (energies, 2, order, order)
    dma = pltpu.SemaphoreType.DMA
    return pl.pallas_call(
        functools.partial(kernel, n, slabs),
        out_shape=[jax.ShapeDtypeStruct(shape, F32)] * 2,
        in_specs=[smem, smem, smem, vmem, vmem, vmem, vmem],
        out_specs=[vmem, vmem],
        scratch_shapes=[
            pltpu.VMEM((2, 2, order, order), F32),
            pltpu.VMEM((9,) + block, F32),
            pltpu.VMEM((2, order, order), F32),
            pltpu.VMEM((2 * order, 6 * order), BF16),
            pltpu.VMEM((6 * order, order), BF16),
            pltpu.VMEM((2 * order, 6 * order), BF16),
            pltpu.VMEM((6 * order, order), BF16),
            pltpu.VMEM((2,) + block, F32),
            pltpu.VMEM((2,) + block, F32),
            pltpu.VMEM((2,) + block, F32),
            pltpu.VMEM(block, F32),
            pltpu.VMEM(block, F32),
            pltpu.SemaphoreType.REGULAR,
            dma,
            dma,
            dma((3, energies)),
            dma((3, energies)),
            dma((2, CHUNKS)),
            dma((2, CHUNKS)),
            dma((2, CHUNKS)),
            dma((2, CHUNKS)),
            dma((2, CHUNKS)),
            dma((2, CHUNKS)),
        ],
        compiler_params=pltpu.CompilerParams(
            collective_id=0, has_side_effects=True, vmem_limit_bytes=60 * 2**20
        ),
    )(energy_real, energy_imag, table, potential, onsite[0], coupling[0], deform[0])


def solution(mesh):
    return jax.shard_map(
        functools.partial(on_device, mesh.shape["energy"], mesh.shape["slab"]),
        mesh=mesh,
        in_specs=(
            P("energy"),
            P("energy"),
            P("slab", None),
            P("slab", None, None, None),
            P("slab", None, None, None),
            P("slab", None, None),
            P(),
            P(),
        ),
        out_specs=(P("energy", "slab", None, None, None), P("energy", "slab", None, None, None)),
        check_vma=False,
    )
```

```python
import functools

import jax
import jax.numpy as jnp
from jax import lax
from jax.experimental import pallas as pl
from jax.experimental.pallas import tpu as pltpu
from jax.sharding import PartitionSpec as P

MESH = pl.DeviceIdType.MESH
CHUNKS = 8
AHEAD = 3
F32 = jnp.float32
BF16 = jnp.bfloat16


def split(value):
    high = value.astype(BF16)
    return high, (value - high.astype(F32)).astype(BF16)


def put_left(ref, real, imag):
    order = real.shape[0]
    real_high, real_low = split(real)
    imag_high, imag_low = split(imag)
    parts = (real_high, real_high, real_low, imag_high, imag_high, imag_low)
    for place in range(6):
        ref[:, place * order : (place + 1) * order] = parts[place]


def put_right(ref, real, imag):
    order = real.shape[0]
    real_high, real_low = split(real)
    imag_high, imag_low = split(imag)
    first = (real_high, real_low, real_high, -imag_high, -imag_low, -imag_high)
    second = (imag_high, imag_low, imag_high, real_high, real_low, real_high)
    for place in range(6):
        cut = slice(place * order, (place + 1) * order)
        ref[cut, :order] = first[place]
        ref[cut, order:] = second[place]


def product(left, right):
    both = jnp.dot(left[...], right[...], preferred_element_type=F32)
    order = left.shape[0]
    return both[:, :order], both[:, order:]


def kernel(
    n, slabs, er_ref, ei_ref, table_ref, potential_ref, onsite_ref, coupling_ref, deform_ref,
    green_ref, sigma_ref,
    base_ref, big, couple, c_left, c_right, left, right, pair, from_low, from_high, to_low, to_high,
    go, base_send, base_recv, slot_send, slot_recv, pair_send, pair_recv, low_send, low_recv, high_send, high_recv,
):
    energies = er_ref.shape[0]
    order = base_ref.shape[-1]
    rows = order // CHUNKS
    me = lax.axis_index("energy")
    q = lax.axis_index("slab")
    side = lax.rem(me, 2)
    partner = me + 1 - 2 * side
    has_low, has_high = me >= 2, me + 2 < n

    def at(energy, slab):
        return {"energy": energy, "slab": slab}

    barrier = pltpu.get_barrier_semaphore()

    def greet(present, energy, slab):
        @pl.when(present)
        def _():
            pl.semaphore_signal(barrier, inc=1, device_id=at(energy, slab), device_id_type=MESH)

    pl.semaphore_signal(barrier, inc=1, device_id=at(partner, q), device_id_type=MESH)
    greet(has_low, me - 2, q)
    greet(has_high, me + 2, q)
    greet(q >= 1, me, q - 1)
    greet(q + 1 < slabs, me, q + 1)

    identity_mask = lax.broadcasted_iota(jnp.int32, (order, order), 0) == lax.broadcasted_iota(
        jnp.int32, (order, order), 1
    )
    middle = max(slabs - 2, 1)
    base_ref[0, 0] = jnp.where(identity_mask, -potential_ref[...] - onsite_ref[0], -onsite_ref[0])
    base_ref[0, 1] = -onsite_ref[1]
    sigma_ref[...] = jnp.zeros_like(sigma_ref)
    put_left(c_left, coupling_ref[0], coupling_ref[1])
    put_right(c_right, coupling_ref[0].T, -coupling_ref[1].T)

    peers = 1
    for present in (has_low, has_high, q >= 1, q + 1 < slabs):
        peers = peers + jnp.where(present, 1, 0)
    pl.semaphore_wait(barrier, peers)

    base_copy = pltpu.make_async_remote_copy(
        src_ref=base_ref.at[0],
        dst_ref=base_ref.at[1],
        send_sem=base_send,
        recv_sem=base_recv,
        device_id=at(me, lax.rem(q + 1, slabs)),
        device_id_type=MESH,
    )

    @pl.when((q >= 1) & (q + 1 <= middle))
    def _():
        base_copy.start()

    @pl.when((q >= 2) & (q <= middle))
    def _():
        base_copy.wait_recv()

    def slot_copy(source, slot, energy):
        return pltpu.make_async_remote_copy(
            src_ref=big.at[source, energy],
            dst_ref=big.at[6 + slot, energy],
            send_sem=slot_send.at[slot, energy],
            recv_sem=slot_recv.at[slot, energy],
            device_id=at(me, lax.rem(q + 1, slabs)),
            device_id_type=MESH,
        )

    def compute(outer, sweep, energy):
        local = (outer == 0) & (sweep == 1) & (q >= 2)
        held = (outer == 1) & (sweep == 0)
        source = jnp.where(local, 0, 6 + outer * sweep)
        coupled = (q >= 1) & jnp.logical_not((outer == 0) & (sweep == 0))

        @pl.when(coupled & jnp.logical_not(local | held))
        def _():
            slot_copy(0, outer * sweep, energy).wait_recv()

        @pl.when(coupled)
        def _():
            put_right(right, big[source, energy, 0], big[source, energy, 1])
            put_left(left, *product(c_left, right))
            couple[0], couple[1] = product(left, c_right)

        @pl.when(jnp.logical_not(coupled))
        def _():
            couple[...] = jnp.zeros_like(couple)

        which = jnp.where((outer == 0) & (sweep == 0), 1, 0)
        ar = base_ref[which, 0] - sigma_ref[energy, 0, 0] - couple[0]
        ai = base_ref[which, 1] - sigma_ref[energy, 0, 1] - couple[1]
        dr = jnp.where(identity_mask, ar + er_ref[energy], 0.0)
        di = jnp.where(identity_mask, ai + ei_ref[energy], 0.0)

        def reciprocal(axis):
            r, i = jnp.sum(dr, axis=axis, keepdims=True), jnp.sum(di, axis=axis, keepdims=True)
            modulus = r * r + i * i
            return r / modulus, -i / modulus

        col_r, col_i = reciprocal(0)
        row_r, row_i = reciprocal(1)
        off_r = jnp.where(identity_mask, 0.0, ar)
        off_i = jnp.where(identity_mask, 0.0, ai)
        w_r = off_r * col_r - off_i * col_i
        w_i = off_r * col_i + off_i * col_r
        couple[0], couple[1] = w_r, w_i
        put_left(left, w_r, w_i)
        put_right(right, w_r, w_i)
        s_r, s_i = product(left, right)
        couple[0] = s_r - couple[0] + jnp.where(identity_mask, 1.0, 0.0)
        couple[1] = s_i - couple[1]
        put_right(right, s_r, s_i)
        p_r, p_i = product(left, right)
        y_r, y_i = couple[0] - p_r, couple[1] - p_i
        target = 3 * outer + sweep
        big[target, energy, 0] = row_r * y_r - row_i * y_i
        big[target, energy, 1] = row_r * y_i + row_i * y_r

        slot = jnp.where(outer == 0, 0, sweep + 1)
        first = (outer == 0) & (sweep == 1)
        second = (outer == 1) & (sweep == 0) & (q + 1 <= middle)
        third = (outer == 1) & (sweep == 1)

        @pl.when((q + 1 < slabs) & (first | second | third))
        def _():
            slot_copy(target, slot, energy).start()

    def pair_copy(outer, final, c):
        cut = pl.ds(c * rows, rows)
        return pltpu.make_async_remote_copy(
            src_ref=big.at[final, :, :, cut],
            dst_ref=pair.at[outer, :, :, cut],
            send_sem=pair_send.at[outer, c],
            recv_sem=pair_recv.at[outer, c],
            device_id=at(partner, q),
            device_id_type=MESH,
        )

    def low_copy(outer, c):
        cut = pl.ds(c * rows, rows)
        return pltpu.make_async_remote_copy(
            src_ref=to_low.at[:, :, cut],
            dst_ref=from_high.at[outer, :, :, cut],
            send_sem=low_send.at[outer, c],
            recv_sem=low_recv.at[outer, c],
            device_id=at(lax.rem(me + n - 2, n), q),
            device_id_type=MESH,
        )

    def high_copy(outer, c):
        cut = pl.ds(c * rows, rows)
        return pltpu.make_async_remote_copy(
            src_ref=to_high.at[:, :, cut],
            dst_ref=from_low.at[outer, :, :, cut],
            send_sem=high_send.at[outer, c],
            recv_sem=high_recv.at[outer, c],
            device_id=at(lax.rem(me + 2, n), q),
            device_id_type=MESH,
        )

    zero_at = 4 * energies - 1
    step_to_partner = energies * (1 - 2 * side)
    strip = 8

    def each_strip(c, body):
        def one(index, carry):
            body(pl.ds(pl.multiple_of(c * rows + index * strip, strip), strip))
            return carry

        lax.fori_loop(0, rows // strip, one, 0)

    def exchange(outer):
        final = jnp.where(outer == 0, jnp.where(q >= 2, 2, 1), 3 + jnp.minimum(q, 2))
        yields = (outer == 0) & (q == 0) & (slabs >= 2)

        def start_rest():
            for c in range(AHEAD, CHUNKS):
                pair_copy(outer, final, c).start()

        for c in range(AHEAD):
            pair_copy(outer, final, c).start()
        pl.when(jnp.logical_not(yields))(start_rest)
        for c in range(CHUNKS):
            if c == AHEAD:

                @pl.when(yields)
                def _():
                    pl.semaphore_wait(go, 1)
                    start_rest()

            pair_copy(outer, final, c).wait_recv()
            if c == CHUNKS - 2:

                @pl.when((outer == 0) & (q == 1))
                def _():
                    pl.semaphore_signal(go, inc=1, device_id=at(me, q - 1), device_id_type=MESH)

            def sums(shift, goal, final=final):
                weight = [
                    [
                        [
                            table_ref[zero_at + shift + b - a + extra]
                            for extra in (0, step_to_partner)
                        ]
                        for b in range(energies)
                    ]
                    for a in range(energies)
                ]

                def body(cut):
                    for part in range(2):
                        own = [big[final, b, part, cut] for b in range(energies)]
                        other = [pair[outer, b, part, cut] for b in range(energies)]
                        for a in range(energies):
                            total = weight[a][0][0] * own[0]
                            for b in range(energies):
                                if b:
                                    total = total + weight[a][b][0] * own[b]
                                total = total + weight[a][b][1] * other[b]
                            goal(a, part, cut, total)

                each_strip(c, body)

            def put_high(a, part, cut, value):
                to_high[a, part, cut] = value

            def put_low(a, part, cut, value):
                to_low[a, part, cut] = value

            def put_own(a, part, cut, value):
                sigma_ref[a, 0, part, cut] = value

            @pl.when(has_high)
            def _():
                sums(-2 * energies, put_high)
                high_copy(outer, c).start()

            @pl.when(has_low)
            def _():
                sums(2 * energies, put_low)
                low_copy(outer, c).start()

            sums(0, put_own)

        for c in range(CHUNKS):

            def add(source):
                def body(cut):
                    for a in range(energies):
                        for part in range(2):
                            sigma_ref[a, 0, part, cut] += source[outer, a, part, cut]

                each_strip(c, body)

            @pl.when(has_low)
            def _():
                high_copy(outer, c).wait_recv()
                add(from_low)

            @pl.when(has_high)
            def _():
                low_copy(outer, c).wait_recv()
                add(from_high)

            def scale(cut):
                level = deform_ref[cut]
                for a in range(energies):
                    for part in range(2):
                        sigma_ref[a, 0, part, cut] = level * sigma_ref[a, 0, part, cut]

            each_strip(c, scale)

        for c in range(CHUNKS):
            pair_copy(outer, final, c).wait_send()

            @pl.when(has_high)
            def _():
                high_copy(outer, c).wait_send()

            @pl.when(has_low)
            def _():
                low_copy(outer, c).wait_send()

    def outer_step(outer, carry):
        def step(j, inner):
            paired = (outer == 0) & (j < 2 * energies)
            sweep = jnp.where(paired, lax.rem(j, 2), lax.div(j, energies))
            energy = jnp.where(paired, lax.div(j, 2), lax.rem(j, energies))
            start = ((outer == 0) & (q >= 2) & (q <= middle)) | ((outer == 1) & (q <= 1))
            mid = (q <= middle) & ((outer == 0) | (q >= 1))
            active = (
                ((sweep == 0) & start) | ((sweep == 1) & mid) | ((sweep == 2) & (q >= 2))
            )

            @pl.when(active)
            def _():
                compute(outer, sweep, energy)

            return inner

        lax.fori_loop(0, 3 * energies, step, 0)
        exchange(outer)
        return carry

    lax.fori_loop(0, 2, outer_step, 0)

    final = 3 + jnp.minimum(q, 2)

    def out(index, carry):
        cut = pl.ds(pl.multiple_of(index * 64, 64), 64)
        for a in range(energies):
            for part in range(2):
                green_ref[a, 0, part, cut] = big[final, a, part, cut]
        return carry

    lax.fori_loop(0, order // 64, out, 0)

    def drain(slot, present):
        @pl.when(present & (q + 1 < slabs))
        def _():
            for energy in range(energies):
                slot_copy(0, slot, energy).wait_send()

    drain(0, q <= middle)
    drain(1, q + 1 <= middle)
    drain(2, (q >= 1) & (q <= middle))

    @pl.when((q >= 1) & (q + 1 <= middle))
    def _():
        base_copy.wait_send()


def on_device(n, slabs, energy_real, energy_imag, potential, onsite, coupling, deform, offsets, weights):
    order = onsite.shape[-1]
    energies = energy_real.shape[0]
    gap = jnp.arange(8 * energies - 1, dtype=jnp.int32) - (4 * energies - 1)
    table = jnp.sum(
        jnp.where(gap[:, None] == offsets[None, :], weights.astype(F32)[None, :] / 128.0, 0.0), axis=-1
    )
    shape = (energies, 1, 2, order, order)
    smem = pl.BlockSpec(memory_space=pltpu.SMEM)
    vmem = pl.BlockSpec(memory_space=pltpu.VMEM)
    block = (energies, 2, order, order)
    dma = pltpu.SemaphoreType.DMA
    return pl.pallas_call(
        functools.partial(kernel, n, slabs),
        out_shape=[jax.ShapeDtypeStruct(shape, F32)] * 2,
        in_specs=[smem, smem, smem, vmem, vmem, vmem, vmem],
        out_specs=[vmem, vmem],
        scratch_shapes=[
            pltpu.VMEM((2, 2, order, order), F32),
            pltpu.VMEM((9,) + block, F32),
            pltpu.VMEM((2, order, order), F32),
            pltpu.VMEM((order, 6 * order), BF16),
            pltpu.VMEM((6 * order, 2 * order), BF16),
            pltpu.VMEM((order, 6 * order), BF16),
            pltpu.VMEM((6 * order, 2 * order), BF16),
            pltpu.VMEM((2,) + block, F32),
            pltpu.VMEM((2,) + block, F32),
            pltpu.VMEM((2,) + block, F32),
            pltpu.VMEM(block, F32),
            pltpu.VMEM(block, F32),
            pltpu.SemaphoreType.REGULAR,
            dma,
            dma,
            dma((3, energies)),
            dma((3, energies)),
            dma((2, CHUNKS)),
            dma((2, CHUNKS)),
            dma((2, CHUNKS)),
            dma((2, CHUNKS)),
            dma((2, CHUNKS)),
            dma((2, CHUNKS)),
        ],
        compiler_params=pltpu.CompilerParams(
            collective_id=0, has_side_effects=True, vmem_limit_bytes=60 * 2**20
        ),
    )(energy_real, energy_imag, table, potential, onsite[0], coupling[0], deform[0])


def solution(mesh):
    return jax.shard_map(
        functools.partial(on_device, mesh.shape["energy"], mesh.shape["slab"]),
        mesh=mesh,
        in_specs=(
            P("energy"),
            P("energy"),
            P("slab", None),
            P("slab", None, None, None),
            P("slab", None, None, None),
            P("slab", None, None),
            P(),
            P(),
        ),
        out_specs=(P("energy", "slab", None, None, None), P("energy", "slab", None, None, None)),
        check_vma=False,
    )
```

```python
import functools

import jax
import jax.numpy as jnp
from jax import lax
from jax.experimental import pallas as pl
from jax.experimental.pallas import tpu as pltpu
from jax.sharding import PartitionSpec as P

MESH = pl.DeviceIdType.MESH
CHUNKS = 8
AHEAD = 3
F32 = jnp.float32
BF16 = jnp.bfloat16


def split(value):
    high = value.astype(BF16)
    return high, (value - high.astype(F32)).astype(BF16)


def put_left(ref, real, imag):
    order = real.shape[0]
    real_high, real_low = split(real)
    imag_high, imag_low = split(imag)
    parts = (real_high, real_high, real_low, imag_high, imag_high, imag_low)
    for place in range(6):
        ref[:, place * order : (place + 1) * order] = parts[place]


def put_right(ref, real, imag):
    order = real.shape[0]
    real_high, real_low = split(real)
    imag_high, imag_low = split(imag)
    first = (real_high, real_low, real_high, -imag_high, -imag_low, -imag_high)
    second = (imag_high, imag_low, imag_high, real_high, real_low, real_high)
    for place in range(6):
        cut = slice(place * order, (place + 1) * order)
        ref[cut, :order] = first[place]
        ref[cut, order:] = second[place]


def product(left, right):
    both = jnp.dot(left[...], right[...], preferred_element_type=F32)
    order = both.shape[0]
    return both[:, :order], both[:, order:]


def kernel(
    n, slabs, er_ref, ei_ref, table_ref, potential_ref, onsite_ref, coupling_ref, deform_ref,
    green_ref, sigma_ref,
    base_ref, helped, big, couple, c_left, c_right, left, right, pair, from_low, from_high, to_low, to_high,
    go, base_send, base_recv, slot_send, slot_recv, pair_send, pair_recv, low_send, low_recv, high_send, high_recv,
):
    energies = er_ref.shape[0]
    order = base_ref.shape[-1]
    rows = order // CHUNKS
    me = lax.axis_index("energy")
    q = lax.axis_index("slab")
    side = lax.rem(me, 2)
    partner = me + 1 - 2 * side
    has_low, has_high = me >= 2, me + 2 < n

    def at(energy, slab):
        return {"energy": energy, "slab": slab}

    barrier = pltpu.get_barrier_semaphore()

    def greet(present, energy, slab):
        @pl.when(present)
        def _():
            pl.semaphore_signal(barrier, inc=1, device_id=at(energy, slab), device_id_type=MESH)

    pl.semaphore_signal(barrier, inc=1, device_id=at(partner, q), device_id_type=MESH)
    greet(has_low, me - 2, q)
    greet(has_high, me + 2, q)
    greet(q >= 1, me, q - 1)
    greet(q + 1 < slabs, me, q + 1)
    greet(q >= 2, me, q - 2)
    greet(q + 2 < slabs, me, q + 2)

    identity_mask = lax.broadcasted_iota(jnp.int32, (order, order), 0) == lax.broadcasted_iota(
        jnp.int32, (order, order), 1
    )
    middle = max(slabs - 2, 1)
    base_ref[0, 0] = jnp.where(identity_mask, -potential_ref[...] - onsite_ref[0], -onsite_ref[0])
    base_ref[0, 1] = -onsite_ref[1]
    sigma_ref[...] = jnp.zeros_like(sigma_ref)
    put_left(c_left.at[0], coupling_ref[0], coupling_ref[1])
    put_right(c_right.at[0], coupling_ref[0].T, -coupling_ref[1].T)

    peers = 1
    for present in (has_low, has_high, q >= 1, q + 1 < slabs, q >= 2, q + 2 < slabs):
        peers = peers + jnp.where(present, 1, 0)
    pl.semaphore_wait(barrier, peers)

    half = energies // 2

    def early(source, goal, place, by):
        return pltpu.make_async_remote_copy(
            src_ref=source,
            dst_ref=goal,
            send_sem=base_send.at[place],
            recv_sem=base_recv.at[place],
            device_id=at(me, lax.rem(q + by, slabs)),
            device_id_type=MESH,
        )

    near = early(base_ref.at[0], base_ref.at[1], 0, 1)
    far = early(base_ref.at[0], base_ref.at[1], 1, 2)
    beside = early(base_ref.at[0], base_ref.at[2], 2, 1)
    lent = early(coupling_ref, helped, 3, 1)
    gives_far = (q >= 1) & (q + 1 <= middle)
    gives_near = (q >= 2) & (q <= middle)

    @pl.when(gives_far)
    def _():
        near.start()
        far.start()

    @pl.when(gives_near)
    def _():
        beside.start()
        lent.start()
        near.wait_recv()

    @pl.when(q >= 3)
    def _():
        lent.wait_recv()
        put_left(c_left.at[1], helped[0], helped[1])
        put_right(c_right.at[1], helped[0].T, -helped[1].T)
        beside.wait_recv()
        far.wait_recv()

    def slot_copy(source, slot, energy):
        return pltpu.make_async_remote_copy(
            src_ref=big.at[source, energy],
            dst_ref=big.at[6 + slot, energy],
            send_sem=slot_send.at[slot, energy],
            recv_sem=slot_recv.at[slot, energy],
            device_id=at(me, lax.rem(q + 1, slabs)),
            device_id_type=MESH,
        )

    def compute(outer, sweep, energy):
        local = (outer == 0) & (sweep == 1) & (q >= 2)
        held = (outer == 1) & (sweep == 0)
        helper = (outer == 0) & (sweep == 1) & (q >= 3)
        own = (outer == 0) & (sweep == 2) & (q >= 3) & (energy >= half)
        lender = jnp.where(helper, 1, 0)
        source = jnp.where(local, 0, 6 + outer * sweep)
        coupled = (q >= 1) & jnp.logical_not((outer == 0) & (sweep == 0))

        @pl.when(coupled & jnp.logical_not(local | held | own))
        def _():
            slot_copy(0, outer * sweep, energy).wait_recv()

        @pl.when(coupled)
        def _():
            put_right(right, big[source, energy, 0], big[source, energy, 1])
            put_left(left, *product(c_left.at[lender], right))
            couple[0], couple[1] = product(left, c_right.at[lender])

        @pl.when(jnp.logical_not(coupled))
        def _():
            couple[...] = jnp.zeros_like(couple)

        which = jnp.where((outer == 0) & (sweep == 0), 1, 2 * lender)
        ar = base_ref[which, 0] - sigma_ref[energy, 0, 0] - couple[0]
        ai = base_ref[which, 1] - sigma_ref[energy, 0, 1] - couple[1]
        dr = jnp.where(identity_mask, ar + er_ref[energy], 0.0)
        di = jnp.where(identity_mask, ai + ei_ref[energy], 0.0)

        def reciprocal(axis):
            r, i = jnp.sum(dr, axis=axis, keepdims=True), jnp.sum(di, axis=axis, keepdims=True)
            modulus = r * r + i * i
            return r / modulus, -i / modulus

        col_r, col_i = reciprocal(0)
        row_r, row_i = reciprocal(1)
        off_r = jnp.where(identity_mask, 0.0, ar)
        off_i = jnp.where(identity_mask, 0.0, ai)
        w_r = off_r * col_r - off_i * col_i
        w_i = off_r * col_i + off_i * col_r
        couple[0], couple[1] = w_r, w_i
        put_left(left, w_r, w_i)
        put_right(right, w_r, w_i)
        s_r, s_i = product(left, right)
        couple[0] = s_r - couple[0] + jnp.where(identity_mask, 1.0, 0.0)
        couple[1] = s_i - couple[1]
        put_right(right, s_r, s_i)
        p_r, p_i = product(left, right)
        y_r, y_i = couple[0] - p_r, couple[1] - p_i
        target = jnp.where(helper, 6, 3 * outer + sweep)
        big[target, energy, 0] = row_r * y_r - row_i * y_i
        big[target, energy, 1] = row_r * y_i + row_i * y_r

        slot = jnp.where(outer == 0, 0, sweep + 1)
        first = (outer == 0) & (sweep == 1)
        second = (outer == 1) & (sweep == 0) & (q + 1 <= middle)
        third = (outer == 1) & (sweep == 1)

        @pl.when((q + 1 < slabs) & (first | second | third))
        def _():
            slot_copy(target, slot, energy).start()

    def pair_copy(outer, final, c):
        cut = pl.ds(c * rows, rows)
        return pltpu.make_async_remote_copy(
            src_ref=big.at[final, :, :, cut],
            dst_ref=pair.at[outer, :, :, cut],
            send_sem=pair_send.at[outer, c],
            recv_sem=pair_recv.at[outer, c],
            device_id=at(partner, q),
            device_id_type=MESH,
        )

    def low_copy(outer, c):
        cut = pl.ds(c * rows, rows)
        return pltpu.make_async_remote_copy(
            src_ref=to_low.at[:, :, cut],
            dst_ref=from_high.at[outer, :, :, cut],
            send_sem=low_send.at[outer, c],
            recv_sem=low_recv.at[outer, c],
            device_id=at(lax.rem(me + n - 2, n), q),
            device_id_type=MESH,
        )

    def high_copy(outer, c):
        cut = pl.ds(c * rows, rows)
        return pltpu.make_async_remote_copy(
            src_ref=to_high.at[:, :, cut],
            dst_ref=from_low.at[outer, :, :, cut],
            send_sem=high_send.at[outer, c],
            recv_sem=high_recv.at[outer, c],
            device_id=at(lax.rem(me + 2, n), q),
            device_id_type=MESH,
        )

    zero_at = 4 * energies - 1
    step_to_partner = energies * (1 - 2 * side)
    strip = 8

    def each_strip(c, body):
        def one(index, carry):
            body(pl.ds(pl.multiple_of(c * rows + index * strip, strip), strip))
            return carry

        lax.fori_loop(0, rows // strip, one, 0)

    def exchange(outer):
        final = jnp.where(outer == 0, jnp.where(q >= 2, 2, 1), 3 + jnp.minimum(q, 2))
        yields = (outer == 0) & (q == 0) & (slabs >= 2)

        def start_rest():
            for c in range(AHEAD, CHUNKS):
                pair_copy(outer, final, c).start()

        for c in range(AHEAD):
            pair_copy(outer, final, c).start()
        pl.when(jnp.logical_not(yields))(start_rest)
        for c in range(CHUNKS):
            if c == AHEAD:

                @pl.when(yields)
                def _():
                    pl.semaphore_wait(go, 1)
                    start_rest()

            pair_copy(outer, final, c).wait_recv()
            if c == CHUNKS - 2:

                @pl.when((outer == 0) & (q == 1))
                def _():
                    pl.semaphore_signal(go, inc=1, device_id=at(me, q - 1), device_id_type=MESH)

            def sums(shift, goal, final=final):
                weight = [
                    [
                        [
                            table_ref[zero_at + shift + b - a + extra]
                            for extra in (0, step_to_partner)
                        ]
                        for b in range(energies)
                    ]
                    for a in range(energies)
                ]

                def body(cut):
                    for part in range(2):
                        own = [big[final, b, part, cut] for b in range(energies)]
                        other = [pair[outer, b, part, cut] for b in range(energies)]
                        for a in range(energies):
                            total = weight[a][0][0] * own[0]
                            for b in range(energies):
                                if b:
                                    total = total + weight[a][b][0] * own[b]
                                total = total + weight[a][b][1] * other[b]
                            goal(a, part, cut, total)

                each_strip(c, body)

            def put_high(a, part, cut, value):
                to_high[a, part, cut] = value

            def put_low(a, part, cut, value):
                to_low[a, part, cut] = value

            def put_own(a, part, cut, value):
                sigma_ref[a, 0, part, cut] = value

            @pl.when(has_high)
            def _():
                sums(-2 * energies, put_high)
                high_copy(outer, c).start()

            @pl.when(has_low)
            def _():
                sums(2 * energies, put_low)
                low_copy(outer, c).start()

            sums(0, put_own)

        for c in range(CHUNKS):

            def add(source):
                def body(cut):
                    for a in range(energies):
                        for part in range(2):
                            sigma_ref[a, 0, part, cut] += source[outer, a, part, cut]

                each_strip(c, body)

            @pl.when(has_low)
            def _():
                high_copy(outer, c).wait_recv()
                add(from_low)

            @pl.when(has_high)
            def _():
                low_copy(outer, c).wait_recv()
                add(from_high)

            def scale(cut):
                level = deform_ref[cut]
                for a in range(energies):
                    for part in range(2):
                        sigma_ref[a, 0, part, cut] = level * sigma_ref[a, 0, part, cut]

            each_strip(c, scale)

        for c in range(CHUNKS):
            pair_copy(outer, final, c).wait_send()

            @pl.when(has_high)
            def _():
                high_copy(outer, c).wait_send()

            @pl.when(has_low)
            def _():
                low_copy(outer, c).wait_send()

    def outer_step(outer, carry):
        def step(j, inner):
            paired = (outer == 0) & (j < 2 * energies)
            sweep = jnp.where(paired, lax.rem(j, 2), lax.div(j, energies))
            energy = jnp.where(paired, lax.div(j, 2), lax.rem(j, energies))
            share = ((q >= 2) & (q <= middle) & (energy < half)) | ((q >= 3) & (energy >= half))
            start = jnp.where(outer == 0, share, q <= 1)
            mid = jnp.where(outer == 0, (q <= 1) | share, (q <= middle) & (q >= 1))
            active = (
                ((sweep == 0) & start) | ((sweep == 1) & mid) | ((sweep == 2) & (q >= 2))
            )

            @pl.when(active)
            def _():
                compute(outer, sweep, energy)

            return inner

        lax.fori_loop(0, 3 * energies, step, 0)
        exchange(outer)
        return carry

    lax.fori_loop(0, 2, outer_step, 0)

    final = 3 + jnp.minimum(q, 2)

    def out(index, carry):
        cut = pl.ds(pl.multiple_of(index * 64, 64), 64)
        for a in range(energies):
            for part in range(2):
                green_ref[a, 0, part, cut] = big[final, a, part, cut]
        return carry

    lax.fori_loop(0, order // 64, out, 0)

    def drain(slot, present, low=0, high=energies):
        @pl.when(present & (q + 1 < slabs))
        def _():
            for energy in range(low, high):
                slot_copy(0, slot, energy).wait_send()

    drain(0, q <= middle, 0, half)
    drain(0, (q <= middle) & (q <= 1), half, energies)
    drain(1, q + 1 <= middle)
    drain(2, (q >= 1) & (q <= middle))

    @pl.when(gives_far)
    def _():
        near.wait_send()
        far.wait_send()

    @pl.when(gives_near)
    def _():
        beside.wait_send()
        lent.wait_send()


def on_device(n, slabs, energy_real, energy_imag, potential, onsite, coupling, deform, offsets, weights):
    order = onsite.shape[-1]
    energies = energy_real.shape[0]
    gap = jnp.arange(8 * energies - 1, dtype=jnp.int32) - (4 * energies - 1)
    table = jnp.sum(
        jnp.where(gap[:, None] == offsets[None, :], weights.astype(F32)[None, :] / 128.0, 0.0), axis=-1
    )
    shape = (energies, 1, 2, order, order)
    smem = pl.BlockSpec(memory_space=pltpu.SMEM)
    vmem = pl.BlockSpec(memory_space=pltpu.VMEM)
    block = (energies, 2, order, order)
    dma = pltpu.SemaphoreType.DMA
    return pl.pallas_call(
        functools.partial(kernel, n, slabs),
        out_shape=[jax.ShapeDtypeStruct(shape, F32)] * 2,
        in_specs=[smem, smem, smem, vmem, vmem, vmem, vmem],
        out_specs=[vmem, vmem],
        scratch_shapes=[
            pltpu.VMEM((3, 2, order, order), F32),
            pltpu.VMEM((2, order, order), F32),
            pltpu.VMEM((9,) + block, F32),
            pltpu.VMEM((2, order, order), F32),
            pltpu.VMEM((2, order, 6 * order), BF16),
            pltpu.VMEM((2, 6 * order, 2 * order), BF16),
            pltpu.VMEM((order, 6 * order), BF16),
            pltpu.VMEM((6 * order, 2 * order), BF16),
            pltpu.VMEM((2,) + block, F32),
            pltpu.VMEM((2,) + block, F32),
            pltpu.VMEM((2,) + block, F32),
            pltpu.VMEM(block, F32),
            pltpu.VMEM(block, F32),
            pltpu.SemaphoreType.REGULAR,
            dma((4,)),
            dma((4,)),
            dma((3, energies)),
            dma((3, energies)),
            dma((2, CHUNKS)),
            dma((2, CHUNKS)),
            dma((2, CHUNKS)),
            dma((2, CHUNKS)),
            dma((2, CHUNKS)),
            dma((2, CHUNKS)),
        ],
        compiler_params=pltpu.CompilerParams(
            collective_id=0, has_side_effects=True, vmem_limit_bytes=60 * 2**20
        ),
    )(energy_real, energy_imag, table, potential, onsite[0], coupling[0], deform[0])


def solution(mesh):
    return jax.shard_map(
        functools.partial(on_device, mesh.shape["energy"], mesh.shape["slab"]),
        mesh=mesh,
        in_specs=(
            P("energy"),
            P("energy"),
            P("slab", None),
            P("slab", None, None, None),
            P("slab", None, None, None),
            P("slab", None, None),
            P(),
            P(),
        ),
        out_specs=(P("energy", "slab", None, None, None), P("energy", "slab", None, None, None)),
        check_vma=False,
    )
```

```python
import functools

import jax
import jax.numpy as jnp
from jax import lax
from jax.experimental import pallas as pl
from jax.experimental.pallas import tpu as pltpu
from jax.sharding import PartitionSpec as P

MESH = pl.DeviceIdType.MESH
CHUNKS = 8
F32 = jnp.float32
BF16 = jnp.bfloat16


def split(value):
    high = value.astype(BF16)
    return high, (value - high.astype(F32)).astype(BF16)


def put_left(ref, real, imag):
    order = real.shape[0]
    real_high, real_low = split(real)
    imag_high, imag_low = split(imag)
    parts = (real_high, real_high, real_low, imag_high, imag_high, imag_low)
    for place in range(6):
        ref[:, place * order : (place + 1) * order] = parts[place]


def put_right(ref, real, imag):
    order = real.shape[0]
    real_high, real_low = split(real)
    imag_high, imag_low = split(imag)
    first = (real_high, real_low, real_high, -imag_high, -imag_low, -imag_high)
    second = (imag_high, imag_low, imag_high, real_high, real_low, real_high)
    for place in range(6):
        cut = slice(place * order, (place + 1) * order)
        ref[cut, :order] = first[place]
        ref[cut, order:] = second[place]


def product(left, right):
    both = jnp.dot(left[...], right[...], preferred_element_type=F32)
    order = left.shape[0]
    return both[:, :order], both[:, order:]


def kernel(
    n, slabs, er_ref, ei_ref, table_ref, potential_ref, onsite_ref, coupling_ref, deform_ref,
    green_ref, sigma_ref,
    base_ref, big, kept, couple, c_left, c_right, left, right, pair, from_low, from_high, to_low, to_high,
    base_send, base_recv, slot_send, slot_recv, pair_send, pair_recv, low_send, low_recv, high_send, high_recv,
):
    energies = er_ref.shape[0]
    order = base_ref.shape[-1]
    rows = order // CHUNKS
    me = lax.axis_index("energy")
    q = lax.axis_index("slab")
    side = lax.rem(me, 2)
    partner = me + 1 - 2 * side
    has_low, has_high = me >= 2, me + 2 < n

    def at(energy, slab):
        return {"energy": energy, "slab": slab}

    barrier = pltpu.get_barrier_semaphore()

    def greet(present, energy, slab):
        @pl.when(present)
        def _():
            pl.semaphore_signal(barrier, inc=1, device_id=at(energy, slab), device_id_type=MESH)

    pl.semaphore_signal(barrier, inc=1, device_id=at(partner, q), device_id_type=MESH)
    greet(has_low, me - 2, q)
    greet(has_high, me + 2, q)
    greet(q >= 1, me, q - 1)
    greet(q + 1 < slabs, me, q + 1)

    identity_mask = lax.broadcasted_iota(jnp.int32, (order, order), 0) == lax.broadcasted_iota(
        jnp.int32, (order, order), 1
    )
    middle = max(slabs - 2, 1)
    base_ref[0, 0] = jnp.where(identity_mask, -potential_ref[...] - onsite_ref[0], -onsite_ref[0])
    base_ref[0, 1] = -onsite_ref[1]
    sigma_ref[...] = jnp.zeros_like(sigma_ref)
    put_left(c_left, coupling_ref[0], coupling_ref[1])
    put_right(c_right, coupling_ref[0].T, -coupling_ref[1].T)

    peers = 1
    for present in (has_low, has_high, q >= 1, q + 1 < slabs):
        peers = peers + jnp.where(present, 1, 0)
    pl.semaphore_wait(barrier, peers)

    base_copy = pltpu.make_async_remote_copy(
        src_ref=base_ref.at[0],
        dst_ref=base_ref.at[1],
        send_sem=base_send,
        recv_sem=base_recv,
        device_id=at(me, lax.rem(q + 1, slabs)),
        device_id_type=MESH,
    )

    @pl.when((q >= 1) & (q + 1 <= middle))
    def _():
        base_copy.start()

    @pl.when((q >= 2) & (q <= middle))
    def _():
        base_copy.wait_recv()

    def slot_copy(source, slot, energy):
        return pltpu.make_async_remote_copy(
            src_ref=big.at[source, energy],
            dst_ref=big.at[6 + slot, energy],
            send_sem=slot_send.at[slot, energy],
            recv_sem=slot_recv.at[slot, energy],
            device_id=at(me, lax.rem(q + 1, slabs)),
            device_id_type=MESH,
        )

    def compute(outer, sweep, energy):
        local = (outer == 0) & (sweep == 1) & (q >= 2)
        held = (outer == 1) & (sweep == 0)
        source = jnp.where(local, 0, 6 + outer * sweep)
        coupled = (q >= 1) & jnp.logical_not((outer == 0) & (sweep == 0))

        @pl.when(coupled & jnp.logical_not(local | held))
        def _():
            slot_copy(0, outer * sweep, energy).wait_recv()

        @pl.when(coupled & held)
        def _():
            couple[...] = kept[energy]

        @pl.when(coupled & jnp.logical_not(held))
        def _():
            put_right(right, big[source, energy, 0], big[source, energy, 1])
            put_left(left, *product(c_left, right))
            couple[0], couple[1] = product(left, c_right)

        @pl.when(coupled & (outer == 0) & (sweep == 1))
        def _():
            kept[energy] = couple[...]

        @pl.when(jnp.logical_not(coupled))
        def _():
            couple[...] = jnp.zeros_like(couple)

        which = jnp.where((outer == 0) & (sweep == 0), 1, 0)
        ar = base_ref[which, 0] - sigma_ref[energy, 0, 0] - couple[0]
        ai = base_ref[which, 1] - sigma_ref[energy, 0, 1] - couple[1]
        dr = jnp.where(identity_mask, ar + er_ref[energy], 0.0)
        di = jnp.where(identity_mask, ai + ei_ref[energy], 0.0)

        def reciprocal(axis):
            r, i = jnp.sum(dr, axis=axis, keepdims=True), jnp.sum(di, axis=axis, keepdims=True)
            modulus = r * r + i * i
            return r / modulus, -i / modulus

        col_r, col_i = reciprocal(0)
        row_r, row_i = reciprocal(1)
        off_r = jnp.where(identity_mask, 0.0, ar)
        off_i = jnp.where(identity_mask, 0.0, ai)
        w_r = off_r * col_r - off_i * col_i
        w_i = off_r * col_i + off_i * col_r
        couple[0], couple[1] = w_r, w_i
        put_left(left, w_r, w_i)
        put_right(right, w_r, w_i)
        s_r, s_i = product(left, right)
        couple[0] = s_r - couple[0] + jnp.where(identity_mask, 1.0, 0.0)
        couple[1] = s_i - couple[1]
        put_right(right, s_r, s_i)
        p_r, p_i = product(left, right)
        y_r, y_i = couple[0] - p_r, couple[1] - p_i
        target = 3 * outer + sweep
        big[target, energy, 0] = row_r * y_r - row_i * y_i
        big[target, energy, 1] = row_r * y_i + row_i * y_r

        slot = jnp.where(outer == 0, 0, sweep + 1)
        first = (outer == 0) & (sweep == 1)
        second = (outer == 1) & (sweep == 0) & (q + 1 <= middle)
        third = (outer == 1) & (sweep == 1)

        @pl.when((q + 1 < slabs) & (first | second | third))
        def _():
            slot_copy(target, slot, energy).start()

    def pair_copy(outer, final, c):
        cut = pl.ds(c * rows, rows)
        return pltpu.make_async_remote_copy(
            src_ref=big.at[final, :, :, cut],
            dst_ref=pair.at[outer, :, :, cut],
            send_sem=pair_send.at[outer, c],
            recv_sem=pair_recv.at[outer, c],
            device_id=at(partner, q),
            device_id_type=MESH,
        )

    def low_copy(outer, c):
        cut = pl.ds(c * rows, rows)
        return pltpu.make_async_remote_copy(
            src_ref=to_low.at[:, :, cut],
            dst_ref=from_high.at[outer, :, :, cut],
            send_sem=low_send.at[outer, c],
            recv_sem=low_recv.at[outer, c],
            device_id=at(lax.rem(me + n - 2, n), q),
            device_id_type=MESH,
        )

    def high_copy(outer, c):
        cut = pl.ds(c * rows, rows)
        return pltpu.make_async_remote_copy(
            src_ref=to_high.at[:, :, cut],
            dst_ref=from_low.at[outer, :, :, cut],
            send_sem=high_send.at[outer, c],
            recv_sem=high_recv.at[outer, c],
            device_id=at(lax.rem(me + 2, n), q),
            device_id_type=MESH,
        )

    zero_at = 4 * energies - 1
    step_to_partner = energies * (1 - 2 * side)
    strip = 8

    def each_strip(c, body):
        def one(index, carry):
            body(pl.ds(pl.multiple_of(c * rows + index * strip, strip), strip))
            return carry

        lax.fori_loop(0, rows // strip, one, 0)

    def exchange(outer):
        final = jnp.where(outer == 0, jnp.where(q >= 2, 2, 1), 3 + jnp.minimum(q, 2))
        for c in range(CHUNKS):
            pair_copy(outer, final, c).start()
        for c in range(CHUNKS):
            pair_copy(outer, final, c).wait_recv()

            def sums(shift, goal, final=final):
                weight = [
                    [
                        [
                            table_ref[zero_at + shift + b - a + extra]
                            for extra in (0, step_to_partner)
                        ]
                        for b in range(energies)
                    ]
                    for a in range(energies)
                ]

                def body(cut):
                    for part in range(2):
                        own = [big[final, b, part, cut] for b in range(energies)]
                        other = [pair[outer, b, part, cut] for b in range(energies)]
                        for a in range(energies):
                            total = weight[a][0][0] * own[0]
                            for b in range(energies):
                                if b:
                                    total = total + weight[a][b][0] * own[b]
                                total = total + weight[a][b][1] * other[b]
                            goal(a, part, cut, total)

                each_strip(c, body)

            def put_high(a, part, cut, value):
                to_high[a, part, cut] = value

            def put_low(a, part, cut, value):
                to_low[a, part, cut] = value

            def put_own(a, part, cut, value):
                sigma_ref[a, 0, part, cut] = value

            @pl.when(has_high)
            def _():
                sums(-2 * energies, put_high)
                high_copy(outer, c).start()

            @pl.when(has_low)
            def _():
                sums(2 * energies, put_low)
                low_copy(outer, c).start()

            sums(0, put_own)

        for c in range(CHUNKS):

            def add(source):
                def body(cut):
                    for a in range(energies):
                        for part in range(2):
                            sigma_ref[a, 0, part, cut] += source[outer, a, part, cut]

                each_strip(c, body)

            @pl.when(has_low)
            def _():
                high_copy(outer, c).wait_recv()
                add(from_low)

            @pl.when(has_high)
            def _():
                low_copy(outer, c).wait_recv()
                add(from_high)

            def scale(cut):
                level = deform_ref[cut]
                for a in range(energies):
                    for part in range(2):
                        sigma_ref[a, 0, part, cut] = level * sigma_ref[a, 0, part, cut]

            each_strip(c, scale)

        for c in range(CHUNKS):
            pair_copy(outer, final, c).wait_send()

            @pl.when(has_high)
            def _():
                high_copy(outer, c).wait_send()

            @pl.when(has_low)
            def _():
                low_copy(outer, c).wait_send()

    def outer_step(outer, carry):
        def step(j, inner):
            paired = (outer == 0) & (j < 2 * energies)
            sweep = jnp.where(paired, lax.rem(j, 2), lax.div(j, energies))
            energy = jnp.where(paired, lax.div(j, 2), lax.rem(j, energies))
            start = ((outer == 0) & (q >= 2) & (q <= middle)) | ((outer == 1) & (q <= 1))
            mid = (q <= middle) & ((outer == 0) | (q >= 1))
            active = (
                ((sweep == 0) & start) | ((sweep == 1) & mid) | ((sweep == 2) & (q >= 2))
            )

            @pl.when(active)
            def _():
                compute(outer, sweep, energy)

            return inner

        lax.fori_loop(0, 3 * energies, step, 0)
        exchange(outer)
        return carry

    lax.fori_loop(0, 2, outer_step, 0)

    final = 3 + jnp.minimum(q, 2)

    def out(index, carry):
        cut = pl.ds(pl.multiple_of(index * 64, 64), 64)
        for a in range(energies):
            for part in range(2):
                green_ref[a, 0, part, cut] = big[final, a, part, cut]
        return carry

    lax.fori_loop(0, order // 64, out, 0)

    def drain(slot, present):
        @pl.when(present & (q + 1 < slabs))
        def _():
            for energy in range(energies):
                slot_copy(0, slot, energy).wait_send()

    drain(0, q <= middle)
    drain(1, q + 1 <= middle)
    drain(2, (q >= 1) & (q <= middle))

    @pl.when((q >= 1) & (q + 1 <= middle))
    def _():
        base_copy.wait_send()


def on_device(n, slabs, energy_real, energy_imag, potential, onsite, coupling, deform, offsets, weights):
    order = onsite.shape[-1]
    energies = energy_real.shape[0]
    gap = jnp.arange(8 * energies - 1, dtype=jnp.int32) - (4 * energies - 1)
    table = jnp.sum(
        jnp.where(gap[:, None] == offsets[None, :], weights.astype(F32)[None, :] / 128.0, 0.0), axis=-1
    )
    shape = (energies, 1, 2, order, order)
    smem = pl.BlockSpec(memory_space=pltpu.SMEM)
    vmem = pl.BlockSpec(memory_space=pltpu.VMEM)
    block = (energies, 2, order, order)
    dma = pltpu.SemaphoreType.DMA
    return pl.pallas_call(
        functools.partial(kernel, n, slabs),
        out_shape=[jax.ShapeDtypeStruct(shape, F32)] * 2,
        in_specs=[smem, smem, smem, vmem, vmem, vmem, vmem],
        out_specs=[vmem, vmem],
        scratch_shapes=[
            pltpu.VMEM((2, 2, order, order), F32),
            pltpu.VMEM((9,) + block, F32),
            pltpu.VMEM(block, F32),
            pltpu.VMEM((2, order, order), F32),
            pltpu.VMEM((order, 6 * order), BF16),
            pltpu.VMEM((6 * order, 2 * order), BF16),
            pltpu.VMEM((order, 6 * order), BF16),
            pltpu.VMEM((6 * order, 2 * order), BF16),
            pltpu.VMEM((2,) + block, F32),
            pltpu.VMEM((2,) + block, F32),
            pltpu.VMEM((2,) + block, F32),
            pltpu.VMEM(block, F32),
            pltpu.VMEM(block, F32),
            dma,
            dma,
            dma((3, energies)),
            dma((3, energies)),
            dma((2, CHUNKS)),
            dma((2, CHUNKS)),
            dma((2, CHUNKS)),
            dma((2, CHUNKS)),
            dma((2, CHUNKS)),
            dma((2, CHUNKS)),
        ],
        compiler_params=pltpu.CompilerParams(
            collective_id=0, has_side_effects=True, vmem_limit_bytes=60 * 2**20
        ),
    )(energy_real, energy_imag, table, potential, onsite[0], coupling[0], deform[0])


def solution(mesh):
    return jax.shard_map(
        functools.partial(on_device, mesh.shape["energy"], mesh.shape["slab"]),
        mesh=mesh,
        in_specs=(
            P("energy"),
            P("energy"),
            P("slab", None),
            P("slab", None, None, None),
            P("slab", None, None, None),
            P("slab", None, None),
            P(),
            P(),
        ),
        out_specs=(P("energy", "slab", None, None, None), P("energy", "slab", None, None, None)),
        check_vma=False,
    )
```
